256 devices in a mesh: seq: 16 (over x, y), exp: 16 (over z, core).
Axes of the slice: x: 4, y: 4, z: 8, core: 2. Of those that a mesh axis runs over, the one named last changes fastest.
Arguments:
- tokens: bfloat16 [65536, 2048], P(('seq', 'exp')), may hold values from -6 to 6
- pick_rows: int32 [256, 48], P('seq'), may hold values from 0 to 255, as said below
- pick_counts: int32 [256], P('seq'), may hold values from 1 to 48, as said below
- expert_ids: int32 [12288, 6], P('seq'), may hold values from 0 to 15, all different within a row; in each aligned block of 48 rows (0 to 47, 48 to 95, ...) at most 26 rows name the same one
- norm_gains: float32 [2, 2048], replicated, may hold values from 0.5 to 1.5
- depth_router: bfloat16 [2048], replicated, may hold values from -0.125 to 0.125
- w_query: bfloat16 [2048, 2048], P(None, 'exp'), may hold values from -0.5 to 0.5
- w_keyval: bfloat16 [2, 2048, 2048], P(None, None, 'exp'), may hold values from -0.125 to 0.125
- w_out: bfloat16 [2048, 2048], P('exp'), may hold values from -0.125 to 0.125
- expert_router: bfloat16 [2048, 16], replicated, may hold values from -0.125 to 0.125
- w_expert: bfloat16 [16, 3, 2048, 1408], P('exp', None, None, 'seq'), may hold values from -0.125 to 0.125
Outputs:
- mixed: bfloat16 [65536, 2048], P(('seq', 'exp'))
- delta: float32 [12288, 2048], P(('seq', 'exp'))
The draws below stay inside these ranges and needn't reach their ends.
Inputs may be any that keep to these rules, and one draw needn't show every extreme that they name: `pick_rows`: row d names rows of device d: its first pick_counts[d] entries are distinct and ascending, the picked tokens; the other entries are further distinct rows of that device and are not used. `pick_counts`: some device fills all of its 48 slots. `expert_ids`: the 6 experts of a slot are distinct; within the 48 slots of one device (aligned blocks of rows) no expert is named more than 26 times, counting unused slots too.
All inputs are finite; a program needn't handle non-finite values.
Results may differ from the reference program's by a relative error of at most 0.023.
Values may be sent and summed in bfloat16 or wider, within the bound.
A program may use at most 128 MiB of HBM per device.

```python
import math
import jax
import jax.numpy as jnp
import numpy as np
from jax import lax

D = 2048
HEADS = 16
HEAD_DIM = 128
TOP = 6
FF = 1408
TOK_DEV = 256
EXPERTS = 16
PICK_DEV = 48
CAP = 26
TOKENS = 65536
PICKS = 12288
N_SEQ = 16
N_EXP = 16


def pick_plan(key):
    devices = N_SEQ * N_EXP
    key_level, key_extra, key_fill, key_perm = jax.random.split(jax.random.fold_in(key, 7), 4)
    unit = max(PICK_DEV // 6, 1)
    level = jax.random.randint(key_level, (N_SEQ, 1), 1, 5)
    extra = jax.random.randint(key_extra, (N_SEQ, N_EXP), 0, 2 * unit + 1)
    counted = jnp.clip(unit * level + extra, 1, PICK_DEV).reshape(-1)
    fullest = jax.random.randint(key_fill, (), 0, devices)
    counted = jnp.where(jnp.arange(devices) == fullest, PICK_DEV, counted)
    perm_keys = jax.random.split(key_perm, devices)

    def one_device(device_key):
        return jax.random.permutation(device_key, TOK_DEV)[:PICK_DEV]
    chosen = jax.vmap(one_device)(perm_keys)
    live = jnp.arange(PICK_DEV)[None, :] < counted[:, None]
    ordered = jnp.sort(jnp.where(live, chosen, chosen + TOK_DEV), axis=1)
    rows = jnp.where(ordered < TOK_DEV, ordered, ordered - TOK_DEV)
    return (rows.astype(jnp.int32), counted.astype(jnp.int32))


def draw_pick_rows(key, part):
    rows, counted = pick_plan(key)
    return rows


def draw_pick_counts(key, part):
    rows, counted = pick_plan(key)
    return counted


def levels(key, shape, pieces, least, high):
    factor_of, own = 1.0, jax.random.fold_in(key, 6)
    for dim, parts in pieces:
        heights = jnp.exp(jax.random.uniform(jax.random.fold_in(own, dim), (parts,), jnp.float32, least / len(pieces), high / len(pieces)))
        factor_of = factor_of * jnp.repeat(heights, shape[dim] // parts).reshape([-1 if axis == dim else 1 for axis in range(len(shape))])
    return factor_of


def assign_block(rng, own, number, rows, number_of, top, most, lean):
    order = jax.random.permutation(rng, number_of)
    heavy_load, ordinary = load_shares(number_of, rows * top, most, lean, True), load_shares(number_of, rows * top, most, lean, False)
    places = jnp.arange(number_of)

    def named(tallies, turn):
        used = int((tallies > 0).sum())
        fixed = max(1, used // 4)
        moved = fixed + (places - fixed + turn * (used - fixed)) % max(1, number_of - fixed)
        return jnp.zeros((number_of,), jnp.int32).at[order[jnp.where(places < fixed, places, moved)]].set(jnp.asarray(tallies, jnp.int32))

    tallies = jnp.where(number % 4 == 0, named(heavy_load, number // 4), named(ordinary, number - number // 4 - 1))
    mixed = jax.random.permutation(jax.random.fold_in(own, 3), number_of)
    donor, receiver = mixed[0:number_of // 2 * 2:2], mixed[1:number_of // 2 * 2:2]
    slack = jnp.minimum(tallies[donor] - 1, most - tallies[receiver]) // 2
    slack = jnp.where((donor == order[0]) | (receiver == order[0]) | (tallies[receiver] == 0), 0, jnp.maximum(slack, 0))
    moved = jax.random.randint(jax.random.fold_in(own, 4), (number_of // 2,), 0, 1 << 20) % (slack + 1)
    tallies = tallies.at[donor].add(-moved).at[receiver].add(moved)
    items = jnp.searchsorted(jnp.cumsum(tallies), jnp.arange(rows * top), side="right").astype(jnp.int32)
    table = items.reshape(top, rows).T
    table = table[jax.random.permutation(jax.random.fold_in(own, 1), rows)]
    turn = jax.random.randint(jax.random.fold_in(own, 2), (rows, 1), 0, top)
    return jnp.take_along_axis(table, (jnp.arange(top)[None, :] + turn) % top, axis=1)


def load_shares(number_of, total, bound, lean, full):
    portions = [(1 << 20) // math.isqrt(grade ** lean) + 1 for grade in range(1, number_of + 1)]
    largest = bound if full else min(bound, max(-(-total // number_of), total * portions[0] // sum(portions)))
    least = 1 if total - largest >= number_of - 1 else 0
    counts, rest = [largest] + [least] * (number_of - 1), total - largest - least * (number_of - 1)
    while rest > 0:
        candidates = [i for i in range(1, number_of) if counts[i] < largest] or [i for i in range(1, number_of) if counts[i] < bound]
        whole, remaining = sum([portions[i] for i in candidates]), rest
        for i in candidates:
            more = min(bound - counts[i], max(1, remaining * portions[i] // whole), rest)
            counts[i] = counts[i] + more
            rest = rest - more
    return np.array(counts)


def noise(rng, dims, width, bound, cuts=(), kind=jnp.bfloat16):
    level = levels(rng, dims, cuts, -0.22, 0.18) if cuts else 1.0
    values = jax.random.normal(rng, dims, jnp.float32) * width * level
    return jnp.minimum(jnp.maximum(values, -bound), bound).astype(kind)


def setup_inputs(seed: int = 0) -> dict:
    splits = jax.random.split(jax.random.key(seed), 12)
    tokens = noise(splits[0], (TOKENS, D), 1.0, 6.0, ((0, 256),))
    pick_rows = draw_pick_rows(jax.random.fold_in(splits[11], 71), 0)
    pick_counts = draw_pick_counts(jax.random.fold_in(splits[11], 71), 0)
    expert_ids_keys = jax.random.split(jax.random.fold_in(splits[3], 1), PICKS // PICK_DEV)
    expert_ids_turns = jax.random.permutation(jax.random.fold_in(splits[3], 3), PICKS // PICK_DEV)
    expert_ids = jax.vmap(lambda own, number: assign_block(jax.random.fold_in(splits[3], 2), own, number, PICK_DEV, EXPERTS, TOP, CAP, 2))(expert_ids_keys, expert_ids_turns).reshape((PICKS, TOP))
    norm_gains = jnp.clip(1.0 + 0.1 * jax.random.normal(splits[4], (2, D), jnp.float32), 0.5, 1.5)
    depth_router = noise(splits[5], (D,), D ** -0.5, 0.125)
    w_query = noise(splits[6], (D, HEADS * HEAD_DIM), (D // 16) ** -0.5, 0.5, ((1, 16),))
    w_keyval = noise(splits[7], (2, D, HEADS * HEAD_DIM), D ** -0.5, 0.125, ((2, 16),))
    w_out = noise(splits[8], (HEADS * HEAD_DIM, D), (HEADS * HEAD_DIM) ** -0.5, 0.125, ((0, 16),))
    expert_router = noise(splits[9], (D, EXPERTS), D ** -0.5, 0.125)
    w_expert = noise(splits[10], (EXPERTS, 3, D, FF), D ** -0.5, 0.125, ((0, 16), (3, 16)))
    return {"tokens": tokens, "pick_rows": pick_rows, "pick_counts": pick_counts, "expert_ids": expert_ids, "norm_gains": norm_gains, "depth_router": depth_router, "w_query": w_query, "w_keyval": w_keyval, "w_out": w_out, "expert_router": expert_router, "w_expert": w_expert}


far_position = 1 << 30
softcap_limit = 20.0

def normalize(values, gain):
    widened = values.astype(jnp.float32)
    scale = lax.rsqrt(lax.optimization_barrier(jnp.mean(widened * widened, axis=-1, keepdims=True)) + 1e-06)
    return (widened * scale * gain).astype(jnp.bfloat16)

def soft_limit(scores):
    return softcap_limit * jnp.tanh(scores / softcap_limit)

def expert_apply(inputs, matrices):
    gated = jnp.dot(inputs, matrices[0], preferred_element_type=jnp.float32)
    upward = jnp.dot(inputs, matrices[1], preferred_element_type=jnp.float32)
    hidden = (jax.nn.silu(gated) * upward).astype(jnp.bfloat16)
    result = lax.dot_general(hidden, matrices[2], (((1,), (1,)), ((), ())), preferred_element_type=jnp.float32)
    return result.astype(jnp.bfloat16)

def route_weights(normed, router, chosen_ids):
    scores = jax.nn.sigmoid(jnp.dot(normed, router, preferred_element_type=jnp.float32))
    onehot = chosen_ids[:, :, None] == jnp.arange(router.shape[1], dtype=jnp.int32)[None, None, :]
    picked_scores = lax.optimization_barrier(jnp.sum(jnp.where(onehot, scores[:, None, :], jnp.float32(0.0)), axis=-1))
    return picked_scores / lax.optimization_barrier(jnp.sum(picked_scores, axis=-1, keepdims=True))

def attention(queries, keys, values, positions, valid):
    total_rows = queries.shape[0]
    span = total_rows // N_SEQ
    scale = HEAD_DIM ** (-0.5)

    def split_heads(array):
        return array.reshape(N_SEQ, span, HEADS, HEAD_DIM).transpose(2, 0, 1, 3)
    pos_blocks = positions.reshape(N_SEQ, span)
    live_blocks = valid.reshape(N_SEQ, span)

    def one_head(packed):
        head_queries, head_keys, head_values = packed

        def one_block(block_no):
            query_block = head_queries[block_no]
            query_pos = pos_blocks[block_no]

            def step(key_no, carry):

                def add_block(inner):
                    total, mass = inner
                    scores = jnp.dot(query_block, head_keys[key_no].T, preferred_element_type=jnp.float32) * scale
                    allowed = (pos_blocks[key_no][None, :] <= query_pos[:, None]) & live_blocks[key_no][None, :]
                    weight = jnp.where(allowed, jnp.exp(soft_limit(scores)), jnp.float32(0.0))
                    mass = mass + lax.optimization_barrier(jnp.sum(weight, axis=1))
                    total = total + jnp.dot(weight.astype(jnp.bfloat16), head_values[key_no], preferred_element_type=jnp.float32)
                    return (total, mass)

                def keep_block(inner):
                    return inner
                return lax.cond(key_no <= block_no, add_block, keep_block, carry)
            start_carry = (jnp.zeros((span, HEAD_DIM), jnp.float32), jnp.zeros((span,), jnp.float32))
            total, mass = lax.fori_loop(0, N_SEQ, step, start_carry)
            safe_mass = jnp.where(mass > 0, mass, jnp.float32(1.0))
            return (total / safe_mass[:, None]).astype(jnp.bfloat16)
        return lax.map(one_block, jnp.arange(N_SEQ, dtype=jnp.int32))
    heads_out = lax.map(one_head, (split_heads(queries), split_heads(keys), split_heads(values)))
    return heads_out.transpose(1, 2, 0, 3).reshape(total_rows, HEADS * HEAD_DIM)

def expert_mixture(normed, chosen_ids, valid, shares, w_expert):
    total_rows = normed.shape[0]
    span = total_rows // N_SEQ
    row_numbers = jnp.arange(total_rows, dtype=jnp.int32)

    def per_expert(expert, accum):
        matched = (chosen_ids == expert) & valid[:, None]
        share = lax.optimization_barrier(jnp.sum(jnp.where(matched, shares, jnp.float32(0.0)), axis=1))
        routed = jnp.any(matched, axis=1)
        ranking = jnp.argsort(jnp.where(routed, row_numbers, total_rows + row_numbers)).astype(jnp.int32)
        routed_count = jnp.sum(routed.astype(jnp.int32))
        matrices = w_expert[expert]

        def per_block(block_no, inner):
            first = block_no * span

            def compute(current):
                members = lax.dynamic_slice_in_dim(ranking, first, span)
                outputs = expert_apply(normed[members], matrices)
                return current.at[members].add(share[members][:, None] * outputs.astype(jnp.float32))

            def keep_block(current):
                return current
            return lax.cond(first < routed_count, compute, keep_block, inner)
        return lax.fori_loop(0, N_SEQ, per_block, accum)
    return lax.fori_loop(0, EXPERTS, per_expert, jnp.zeros(normed.shape, jnp.float32))

def reference(tokens, pick_rows, pick_counts, expert_ids, norm_gains, depth_router, w_query, w_keyval, w_out, expert_router, w_expert):
    devices = N_SEQ * N_EXP
    slot_range = jnp.arange(PICK_DEV, dtype=jnp.int32)
    valid = (slot_range[None, :] < pick_counts[:, None]).reshape(-1)
    global_rows = (jnp.arange(devices, dtype=jnp.int32)[:, None] * TOK_DEV + pick_rows).reshape(-1).astype(jnp.int32)
    positions = jnp.where(valid, global_rows, far_position).astype(jnp.int32)
    picked = tokens[global_rows]
    normed = normalize(picked, norm_gains[0])
    queries = jnp.dot(normed, w_query, preferred_element_type=jnp.float32).astype(jnp.bfloat16)
    keys = jnp.dot(normed, w_keyval[0], preferred_element_type=jnp.float32).astype(jnp.bfloat16)
    values = jnp.dot(normed, w_keyval[1], preferred_element_type=jnp.float32).astype(jnp.bfloat16)
    attended = attention(queries, keys, values, positions, valid)
    group_width = HEADS * HEAD_DIM // N_EXP
    head_sum = jnp.zeros((picked.shape[0], D), jnp.float32)
    for group in range(N_EXP):
        partial_sum = jnp.dot(attended[:, group * group_width:(group + 1) * group_width], w_out[group * group_width:(group + 1) * group_width], preferred_element_type=jnp.float32)
        partial_sum = lax.optimization_barrier(partial_sum.astype(jnp.bfloat16)).astype(jnp.float32)
        head_sum = head_sum + partial_sum
    mixed_in = normalize(picked.astype(jnp.float32) + head_sum, norm_gains[1])
    shares = route_weights(mixed_in, expert_router, expert_ids)
    mixture = expert_mixture(mixed_in, expert_ids, valid, shares, w_expert)
    delta = jnp.where(valid[:, None], head_sum + mixture, jnp.float32(0.0))
    gate = jax.nn.sigmoid(jnp.dot(picked, depth_router, preferred_element_type=jnp.float32))
    update = jnp.where(valid[:, None], gate[:, None] * delta, jnp.float32(0.0))
    mixed = tokens.astype(jnp.float32).at[global_rows].add(update).astype(jnp.bfloat16)
    return (mixed, delta)
```

```python
import functools
import math

import jax
import jax.numpy as jnp
from jax import lax
from jax.experimental import pallas as pl
from jax.experimental.pallas import tpu as pltpu
from jax.sharding import PartitionSpec as P

HEAD_DIM = 128
softcap_limit = 20.0
MESH = pl.DeviceIdType.MESH
SIDE = 4
RING = 8
SLOTS = 48
SHARD = 768
WIDTH = 2048
HALF = 1024
QUARTER = 192
VMEM = pl.BlockSpec(memory_space=pltpu.VMEM)


def wrap(value, size):
    return lax.rem(value + size, size)


def hops(direction, half):
    return 4 if (direction > 0) == (half == 0) else 3


def hop_number(direction, half, hop):
    return ((0 if direction > 0 else 1) * 2 + half) * 4 + hop - 1


def at_exp(index):
    return {"exp": index}


def ring_place():
    place = lax.axis_index("exp")
    return lax.div(place, 2), lax.rem(place, 2)


def greet(partners):
    barrier = pltpu.get_barrier_semaphore()
    for partner in partners:
        pl.semaphore_signal(barrier, inc=1, device_id=partner, device_id_type=MESH)
    pl.semaphore_wait(barrier, len(partners))


def ring_partners():
    z, core = ring_place()
    return [
        at_exp(2 * wrap(z + 1, RING) + core),
        at_exp(2 * wrap(z - 1, RING) + core),
        at_exp(2 * z + 1 - core),
    ]


def remote(src, dst, send, recv, target):
    return pltpu.make_async_remote_copy(
        src_ref=src, dst_ref=dst, send_sem=send, recv_sem=recv, device_id=target, device_id_type=MESH
    )


def ring_gather(buf, send, recv, sib_send, sib_recv):
    z, core = ring_place()
    sibling = at_exp(2 * z + 1 - core)

    def part(origin, side, half):
        return buf.at[2 * origin + side, :, pl.ds(half * HALF, HALF)]

    def hop_copy(direction, half, hop, arriving):
        origin = wrap(z - direction * (hop if arriving else hop - 1), RING)
        ref = part(origin, core, half)
        number = hop_number(direction, half, hop)
        return remote(ref, ref, send.at[number], recv.at[number], at_exp(2 * wrap(z + direction, RING) + core))

    def sib_copy(direction, half, hop, arriving):
        origin = wrap(z - direction * hop, RING)
        ref = part(origin, 1 - core if arriving else core, half)
        number = hop_number(direction, half, hop)
        return remote(ref, ref, sib_send.at[number], sib_recv.at[number], sibling)

    def own_copy(arriving):
        ref = buf.at[2 * z + (1 - core if arriving else core)]
        return remote(ref, ref, sib_send.at[16], sib_recv.at[16], sibling)

    lanes = [(1, 0), (-1, 1), (1, 1), (-1, 0)]
    for direction, half in lanes:
        hop_copy(direction, half, 1, False).start()
    own_copy(False).start()
    for hop in range(1, 5):
        for direction, half in lanes:
            if hop <= hops(direction, half):
                hop_copy(direction, half, hop, True).wait_recv()
                if hop < hops(direction, half):
                    hop_copy(direction, half, hop + 1, False).start()
                sib_copy(direction, half, hop, False).start()
    own_copy(True).wait_recv()
    own_copy(False).wait_send()
    for hop in range(1, 5):
        for direction, half in lanes:
            if hop <= hops(direction, half):
                sib_copy(direction, half, hop, True).wait_recv()
                sib_copy(direction, half, hop, False).wait_send()
                hop_copy(direction, half, hop, False).wait_send()


def ring_scatter(part, sib, out_buf, in_buf, total, send, recv, sib_send, sib_recv):
    z, core = ring_place()
    sibling = at_exp(2 * z + 1 - core)

    def sib_copy(offset):
        target = wrap(z + offset, RING)
        return remote(
            part.at[2 * target + 1 - core], sib.at[target], sib_send.at[offset % RING], sib_recv.at[offset % RING], sibling
        )

    def mine(target, half):
        columns = pl.ds(half * HALF, HALF)
        return part[2 * target + core, :, columns].astype(jnp.float32) + sib[target, :, columns].astype(jnp.float32)

    def hop_copy(direction, half, hop):
        number = hop_number(direction, half, hop)
        return remote(
            out_buf.at[number], in_buf.at[number], send.at[number], recv.at[number],
            at_exp(2 * wrap(z + direction, RING) + core),
        )

    order = [4, 3, -3, 2, -2, 1, -1, 0]
    for offset in order:
        sib_copy(offset).start()
    arrived = set()
    lanes = [(1, 0), (-1, 1), (1, 1), (-1, 0)]

    def have(offset):
        if offset % RING not in arrived:
            arrived.add(offset % RING)
            sib_copy(offset).wait_recv()

    for hop in range(1, 5):
        for direction, half in lanes:
            last = hops(direction, half)
            if hop <= last:
                offset = direction * (last - hop + 1)
                have(offset)
                number = hop_number(direction, half, hop)
                value = mine(wrap(z + offset, RING), half)
                if hop > 1:
                    hop_copy(direction, half, hop - 1).wait_recv()
                    value = value + in_buf[number - 1].astype(jnp.float32)
                out_buf[number] = value.astype(jnp.bfloat16)
                hop_copy(direction, half, hop).start()
    have(0)
    for half in range(2):
        value = mine(z, half)
        for direction in (1, -1):
            last = hops(direction, half)
            hop_copy(direction, half, last).wait_recv()
            value = value + in_buf[hop_number(direction, half, last)].astype(jnp.float32)
        total[:, half * HALF : (half + 1) * HALF] = value
    for offset in order:
        sib_copy(offset).wait_send()
    for direction, half in lanes:
        for hop in range(1, hops(direction, half) + 1):
            hop_copy(direction, half, hop).wait_send()


def normalize(widened, gain):
    scale = lax.rsqrt(jnp.mean(widened * widened, axis=-1, keepdims=True) + 1e-06)
    return (widened * scale * gain).astype(jnp.bfloat16)


def live_lanes(counts):
    row = lax.broadcasted_iota(jnp.int32, (SHARD, 16), 0)
    first = lax.broadcasted_iota(jnp.int32, (SHARD, 16), 1) * SLOTS
    spread = jnp.where((row >= first) & (row < first + SLOTS), 1.0, 0.0).astype(jnp.bfloat16)
    block = lax.broadcasted_iota(jnp.int32, (16, 128), 0).astype(jnp.float32)
    count_of = jnp.dot(spread, counts.astype(jnp.bfloat16), preferred_element_type=jnp.float32)
    block_of = jnp.dot(spread, block.astype(jnp.bfloat16), preferred_element_type=jnp.float32)
    slot = lax.broadcasted_iota(jnp.int32, (SHARD, 128), 0).astype(jnp.float32) - block_of * SLOTS
    return jnp.where(slot < count_of, 1.0, 0.0)


def project_kernel(
    tokens, rows, counts, gains, w_query, w_keyval, picked, queries, keyval, buf, send, recv, sib_send, sib_recv
):
    place = lax.axis_index("exp")
    greet(ring_partners())
    mine = rows[pl.ds(place, 1), :]
    onehot = jnp.where(
        lax.broadcasted_iota(jnp.int32, (tokens.shape[0], SLOTS), 0) == mine, 1.0, 0.0
    ).T.astype(jnp.bfloat16)
    chosen = jnp.dot(onehot, tokens[...], preferred_element_type=jnp.float32)
    picked[...] = chosen.astype(jnp.bfloat16)
    buf[place] = normalize(chosen, gains[0:1, :])
    ring_gather(buf, send, recv, sib_send, sib_recv)
    normed = buf[...].reshape(SHARD, WIDTH)
    queries[...] = jnp.dot(normed, w_query[...], preferred_element_type=jnp.float32).astype(jnp.bfloat16)
    keys = jnp.dot(normed, w_keyval[0], preferred_element_type=jnp.float32).astype(jnp.bfloat16)
    values = jnp.dot(normed, w_keyval[1], preferred_element_type=jnp.float32)
    values = (values * live_lanes(counts[...])).astype(jnp.bfloat16)
    keyval[:, :, 0:HEAD_DIM] = keys.reshape(4, QUARTER, HEAD_DIM)
    keyval[:, :, HEAD_DIM:] = values.reshape(4, QUARTER, HEAD_DIM)


def torus_place():
    place = lax.axis_index("seq")
    return lax.div(place, SIDE), lax.rem(place, SIDE)


def attend_kernel(
    queries, keyval, counts, w_out, part, kv, tallies, acc, send, recv, count_send, count_recv
):
    x, y = torus_place()
    seq = lax.axis_index("seq")

    def at(px, py):
        return {"seq": wrap(px, SIDE) * SIDE + wrap(py, SIDE)}

    greet(
        [at(x, y + 1), at(x, y - 1), at(x, y + 2), at(x + 1, y), at(x - 1, y), at(x + 2, y)]
    )

    def shifted(quarter, first, second):
        if quarter < 2:
            return x + second, y + first
        return x + first, y + second

    def slot(quarter, first, second):
        px, py = shifted(quarter, first, second)
        return wrap(px, SIDE) * SIDE + wrap(py, SIDE)

    def flow(quarter):
        return 1 if quarter % 2 == 0 else -1

    def lines(quarter):
        d = flow(quarter)
        return [0, -d, d, -2 * d]

    def arriving(quarter, number):
        d = flow(quarter)
        if number < 3:
            return [(-d, 0), (d, 0), (-2 * d, 0)][number]
        line, kind = divmod(number - 3, 3)
        return lines(quarter)[line], [-d, d, -2 * d][kind]

    def copy(quarter, number, incoming):
        first, second = arriving(quarter, number)
        d = flow(quarter)
        kind = number if number < 3 else (number - 3) % 3
        step = d if kind in (0, 2) else -d
        if not incoming:
            if number < 3:
                first = first + step
            else:
                second = second + step
        ref = kv.at[slot(quarter, first, second), quarter]
        target = shifted(quarter, step, 0) if number < 3 else shifted(quarter, 0, step)
        place = quarter * 15 + number
        return remote(ref, ref, send.at[place], recv.at[place], at(*target))

    def start(quarter, number):
        copy(quarter, number, False).start()

    def arrive(quarter, number):
        copy(quarter, number, True).wait_recv()

    tallies[x, y] = counts[...]
    kv[seq] = keyval[...]
    for quarter in range(4):
        for number in (0, 1, 3, 4):
            start(quarter, number)

    def count_copy(axis, shift, incoming):
        number = (0 if axis == 1 else 3) + shift - 1
        if axis == 1:
            ref = tallies.at[x, wrap(y - shift, SIDE) if incoming else y]
            target = at(x, y + shift)
        else:
            ref = tallies.at[wrap(x - shift, SIDE) if incoming else x]
            target = at(x + shift, y)
        return remote(ref, ref, count_send.at[number], count_recv.at[number], target)

    for shift in (1, 2, 3):
        count_copy(1, shift, False).start()

    c1 = HEAD_DIM ** (-0.5) / softcap_limit
    c2 = softcap_limit * math.log2(math.e)
    tile = 256

    def unit(source_x, source_y, diagonal):
        source = source_x * SIDE + source_y
        keys = kv[source, :, :, 0:HEAD_DIM].reshape(SHARD, HEAD_DIM)
        live = live_lanes(tallies[source_x, source_y]).astype(jnp.bfloat16)
        values = jnp.concatenate([kv[source, :, :, HEAD_DIM:].reshape(SHARD, HEAD_DIM), live], axis=1)

        @pl.loop(0, SHARD // tile)
        def _(number):
            first = pl.multiple_of(number * tile, tile)
            scores = lax.dot_general(
                queries[pl.ds(first, tile), :], keys, (((1,), (1,)), ((), ())), preferred_element_type=jnp.float32
            )
            weight = jnp.exp2(c2 * jnp.tanh(scores * c1))
            if diagonal:
                row = lax.broadcasted_iota(jnp.int32, (tile, SHARD), 0) + first
                column = lax.broadcasted_iota(jnp.int32, (tile, SHARD), 1)
                weight = jnp.where(column <= row, weight, 0.0)
            term = jnp.dot(weight.astype(jnp.bfloat16), values, preferred_element_type=jnp.float32)
            if diagonal:
                acc[pl.ds(first, tile), :] = term
            else:
                acc[pl.ds(first, tile), :] += term

    def earlier(dx, dy):
        px, py = wrap(x + dx, SIDE), wrap(y + dy, SIDE)

        @pl.when(px * SIDE + py < seq)
        def _():
            unit(px, py, False)

    unit(x, y, True)
    for shift in (1, 2, 3):
        count_copy(1, shift, True).wait_recv()
    for shift in (1, 2, 3):
        count_copy(0, shift, False).start()
    for quarter in range(4):
        arrive(quarter, 0)
        start(quarter, 2)
        start(quarter, 6)
        start(quarter, 7)
    for quarter in range(4):
        arrive(quarter, 1)
        start(quarter, 9)
        start(quarter, 10)
        arrive(quarter, 3)
        start(quarter, 5)
        arrive(quarter, 4)
    for shift in (1, 2, 3):
        count_copy(0, shift, True).wait_recv()
    earlier(1, 0)
    earlier(-1, 0)
    for quarter in range(4):
        arrive(quarter, 2)
        start(quarter, 12)
        start(quarter, 13)
    earlier(0, 1)
    earlier(0, -1)
    for quarter in range(4):
        arrive(quarter, 6)
        start(quarter, 8)
        arrive(quarter, 9)
        start(quarter, 11)
    for quarter in range(4):
        arrive(quarter, 7)
        arrive(quarter, 10)
        arrive(quarter, 5)
    earlier(1, 1)
    earlier(1, -1)
    for quarter in range(4):
        arrive(quarter, 12)
        start(quarter, 14)
    earlier(-1, 1)
    earlier(-1, -1)
    earlier(2, 0)
    earlier(0, 2)
    for quarter in range(4):
        arrive(quarter, 13)
        arrive(quarter, 8)
        arrive(quarter, 11)
    earlier(2, 1)
    earlier(2, -1)
    earlier(1, 2)
    earlier(-1, 2)
    for quarter in range(4):
        arrive(quarter, 14)
    earlier(2, 2)

    mass = acc[:, HEAD_DIM:]
    attended = (acc[:, 0:HEAD_DIM] / jnp.where(mass > 0, mass, 1.0)).astype(jnp.bfloat16)
    acc[:, 0:HEAD_DIM] = attended.astype(jnp.float32)
    per = SHARD // 16

    @pl.loop(0, 4)
    def _(number):
        rows = acc[pl.ds(pl.multiple_of(number * 4 * per, 4 * per), 4 * per), 0:HEAD_DIM].astype(jnp.bfloat16)
        result = jnp.dot(rows, w_out[...], preferred_element_type=jnp.float32).astype(jnp.bfloat16)
        part[pl.ds(number * 4, 4)] = result.reshape(4, per, WIDTH)

    for shift in (1, 2, 3):
        count_copy(1, shift, False).wait_send()
        count_copy(0, shift, False).wait_send()
    for quarter in range(4):
        for number in range(15):
            copy(quarter, number, False).wait_send()


def mix_kernel(
    part, picked, gains, head, normed, sib, out_buf, in_buf, buf,
    send, recv, sib_send, sib_recv, send2, recv2, sib_send2, sib_recv2,
):
    place = lax.axis_index("exp")
    greet(ring_partners())
    ring_scatter(part, sib, out_buf, in_buf, head, send, recv, sib_send, sib_recv)
    buf[place] = normalize(picked[...].astype(jnp.float32) + head[...], gains[1:2, :])
    ring_gather(buf, send2, recv2, sib_send2, sib_recv2)
    normed[...] = buf[...].reshape(SHARD, WIDTH)


def return_kernel(part, total, sib, out_buf, in_buf, send, recv, sib_send, sib_recv):
    greet(ring_partners())
    ring_scatter(part, sib, out_buf, in_buf, total, send, recv, sib_send, sib_recv)


def dma(count):
    return pltpu.SemaphoreType.DMA((count,))


def params(number, mib=40):
    return pltpu.CompilerParams(collective_id=number, has_side_effects=True, vmem_limit_bytes=mib << 20)


GATHER_SEMS = [dma(16), dma(16), dma(17), dma(17)]
SCATTER_BUFS = [
    pltpu.VMEM((RING, SLOTS, WIDTH), jnp.bfloat16),
    pltpu.VMEM((16, SLOTS, HALF), jnp.bfloat16),
    pltpu.VMEM((16, SLOTS, HALF), jnp.bfloat16),
]
SCATTER_SEMS = [dma(16), dma(16), dma(8), dma(8)]


def local(
    tokens, pick_rows, pick_counts, expert_ids, norm_gains, depth_router,
    w_query, w_keyval, w_out, expert_router, w_expert,
):
    exp_place = lax.axis_index("exp")
    f32, bf16 = jnp.float32, jnp.bfloat16
    matrices = lax.all_gather(w_expert, "seq", axis=3, tiled=True)[0]
    counts = jnp.broadcast_to(pick_counts.astype(f32)[:, None], (16, 128))
    picked, queries, keyval = pl.pallas_call(
        project_kernel,
        out_shape=(
            jax.ShapeDtypeStruct((SLOTS, WIDTH), bf16),
            jax.ShapeDtypeStruct((SHARD, HEAD_DIM), bf16),
            jax.ShapeDtypeStruct((4, QUARTER, 2 * HEAD_DIM), bf16),
        ),
        in_specs=[VMEM] * 6,
        out_specs=(VMEM,) * 3,
        scratch_shapes=[pltpu.VMEM((16, SLOTS, WIDTH), bf16)] + GATHER_SEMS,
        compiler_params=params(0),
        name="project",
    )(tokens, pick_rows, counts, norm_gains, w_query, w_keyval)
    part = pl.pallas_call(
        attend_kernel,
        out_shape=jax.ShapeDtypeStruct((16, SLOTS, WIDTH), bf16),
        in_specs=[VMEM] * 4,
        out_specs=VMEM,
        scratch_shapes=[
            pltpu.VMEM((16, 4, QUARTER, 2 * HEAD_DIM), bf16),
            pltpu.VMEM((SIDE, SIDE, 16, 128), f32),
            pltpu.VMEM((SHARD, 2 * HEAD_DIM), f32),
            dma(60), dma(60), dma(6), dma(6),
        ],
        compiler_params=params(1),
        name="attend",
    )(queries, keyval, counts, w_out)
    head_mine, normed_all = pl.pallas_call(
        mix_kernel,
        out_shape=(
            jax.ShapeDtypeStruct((SLOTS, WIDTH), f32),
            jax.ShapeDtypeStruct((SHARD, WIDTH), bf16),
        ),
        in_specs=[VMEM] * 3,
        out_specs=(VMEM,) * 2,
        scratch_shapes=SCATTER_BUFS + [pltpu.VMEM((16, SLOTS, WIDTH), bf16)] + SCATTER_SEMS + GATHER_SEMS,
        compiler_params=params(2),
        name="mix",
    )(part, picked, norm_gains)

    experts = expert_router.shape[1]
    named = jnp.any(expert_ids == exp_place, axis=1)
    rank = jnp.cumsum(named.astype(jnp.int32)) - 1
    capacity = 416
    select = jnp.where(
        (rank[None, :] == jnp.arange(capacity, dtype=jnp.int32)[:, None]) & named[None, :], 1.0, 0.0
    ).astype(bf16)
    chosen = jnp.any(
        expert_ids[:, :, None] == jnp.arange(experts, dtype=jnp.int32)[None, None, :], axis=1
    )
    scores = jax.nn.sigmoid(jnp.dot(normed_all, expert_router, preferred_element_type=f32))
    scores = jnp.where(chosen, scores, 0.0)
    share = lax.dynamic_index_in_dim(scores, exp_place, 1, keepdims=False) / jnp.sum(scores, axis=1)
    inputs = jnp.dot(select, normed_all, preferred_element_type=f32).astype(bf16)
    gated = jnp.dot(inputs, matrices[0], preferred_element_type=f32)
    upward = jnp.dot(inputs, matrices[1], preferred_element_type=f32)
    hidden = (jax.nn.silu(gated) * upward).astype(bf16)
    result = lax.dot_general(hidden, matrices[2], (((1,), (1,)), ((), ())), preferred_element_type=f32).astype(bf16)
    spread = lax.dot_general(select, result, (((0,), (0,)), ((), ())), preferred_element_type=f32)
    weighted = (spread * share[:, None]).astype(bf16).reshape(16, SLOTS, WIDTH)
    mixture = pl.pallas_call(
        return_kernel,
        out_shape=jax.ShapeDtypeStruct((SLOTS, WIDTH), f32),
        in_specs=[VMEM],
        out_specs=VMEM,
        scratch_shapes=SCATTER_BUFS + SCATTER_SEMS,
        compiler_params=params(3),
        name="bring_back",
    )(weighted)

    my_rows = lax.dynamic_index_in_dim(pick_rows, exp_place, 0, keepdims=False)
    my_count = lax.dynamic_index_in_dim(pick_counts, exp_place, 0, keepdims=False)
    my_valid = jnp.arange(SLOTS, dtype=jnp.int32) < my_count
    delta = jnp.where(my_valid[:, None], head_mine + mixture, 0.0)
    gate = jax.nn.sigmoid(jnp.dot(picked, depth_router, preferred_element_type=f32))
    update = jnp.where(my_valid[:, None], gate[:, None] * delta, 0.0)
    mixed = tokens.astype(f32).at[my_rows].add(update).astype(bf16)
    return (mixed, delta)


def solution(mesh):
    in_specs = (
        P(("seq", "exp"), None), P("seq", None), P("seq"), P("seq", None), P(), P(),
        P(None, "exp"), P(None, None, "exp"), P("exp", None), P(), P("exp", None, None, "seq"),
    )
    out_specs = (P(("seq", "exp"), None), P(("seq", "exp"), None))
    return jax.shard_map(local, mesh=mesh, in_specs=in_specs, out_specs=out_specs, check_vma=False)
```

```python
import functools
import math

import jax
import jax.numpy as jnp
from jax import lax
from jax.experimental import pallas as pl
from jax.experimental.pallas import tpu as pltpu
from jax.sharding import PartitionSpec as P

HEAD_DIM = 128
softcap_limit = 20.0
MESH = pl.DeviceIdType.MESH
SIDE = 4
RING = 8
SLOTS = 48
SHARD = 768
WIDTH = 2048
HALF = 1024
QUARTER = 192
VMEM = pl.BlockSpec(memory_space=pltpu.VMEM)


def wrap(value, size):
    return lax.rem(value + size, size)


def hops(direction, half):
    return 4 if (direction > 0) == (half == 0) else 3


def hop_number(direction, half, hop):
    return ((0 if direction > 0 else 1) * 2 + half) * 4 + hop - 1


def at_exp(index):
    return {"exp": index}


def ring_place():
    place = lax.axis_index("exp")
    return lax.div(place, 2), lax.rem(place, 2)


def greet(partners):
    barrier = pltpu.get_barrier_semaphore()
    for partner in partners:
        pl.semaphore_signal(barrier, inc=1, device_id=partner, device_id_type=MESH)
    pl.semaphore_wait(barrier, len(partners))


def ring_partners():
    z, core = ring_place()
    return [
        at_exp(2 * wrap(z + 1, RING) + core),
        at_exp(2 * wrap(z - 1, RING) + core),
        at_exp(2 * z + 1 - core),
    ]


def remote(src, dst, send, recv, target):
    return pltpu.make_async_remote_copy(
        src_ref=src, dst_ref=dst, send_sem=send, recv_sem=recv, device_id=target, device_id_type=MESH
    )


def ring_gather(buf, send, recv, sib_send, sib_recv):
    z, core = ring_place()
    sibling = at_exp(2 * z + 1 - core)

    def part(origin, side, half):
        return buf.at[2 * origin + side, :, pl.ds(half * HALF, HALF)]

    def hop_copy(direction, half, hop, arriving):
        origin = wrap(z - direction * (hop if arriving else hop - 1), RING)
        ref = part(origin, core, half)
        number = hop_number(direction, half, hop)
        return remote(ref, ref, send.at[number], recv.at[number], at_exp(2 * wrap(z + direction, RING) + core))

    def sib_copy(direction, half, hop, arriving):
        origin = wrap(z - direction * hop, RING)
        ref = part(origin, 1 - core if arriving else core, half)
        number = hop_number(direction, half, hop)
        return remote(ref, ref, sib_send.at[number], sib_recv.at[number], sibling)

    def own_copy(arriving):
        ref = buf.at[2 * z + (1 - core if arriving else core)]
        return remote(ref, ref, sib_send.at[16], sib_recv.at[16], sibling)

    lanes = [(1, 0), (-1, 1), (1, 1), (-1, 0)]
    for direction, half in lanes:
        hop_copy(direction, half, 1, False).start()
    own_copy(False).start()
    for hop in range(1, 5):
        for direction, half in lanes:
            if hop <= hops(direction, half):
                hop_copy(direction, half, hop, True).wait_recv()
                if hop < hops(direction, half):
                    hop_copy(direction, half, hop + 1, False).start()
                sib_copy(direction, half, hop, False).start()
    own_copy(True).wait_recv()
    own_copy(False).wait_send()
    for hop in range(1, 5):
        for direction, half in lanes:
            if hop <= hops(direction, half):
                sib_copy(direction, half, hop, True).wait_recv()
                sib_copy(direction, half, hop, False).wait_send()
                hop_copy(direction, half, hop, False).wait_send()


def ring_scatter(part, sib, out_buf, in_buf, total, send, recv, sib_send, sib_recv):
    z, core = ring_place()
    sibling = at_exp(2 * z + 1 - core)

    def sib_copy(offset):
        target = wrap(z + offset, RING)
        return remote(
            part.at[2 * target + 1 - core], sib.at[target], sib_send.at[offset % RING], sib_recv.at[offset % RING], sibling
        )

    def mine(target, half):
        columns = pl.ds(half * HALF, HALF)
        return part[2 * target + core, :, columns].astype(jnp.float32) + sib[target, :, columns].astype(jnp.float32)

    def hop_copy(direction, half, hop):
        number = hop_number(direction, half, hop)
        return remote(
            out_buf.at[number], in_buf.at[number], send.at[number], recv.at[number],
            at_exp(2 * wrap(z + direction, RING) + core),
        )

    order = [4, 3, -3, 2, -2, 1, -1, 0]
    for offset in order:
        sib_copy(offset).start()
    arrived = set()
    lanes = [(1, 0), (-1, 1), (1, 1), (-1, 0)]

    def have(offset):
        if offset % RING not in arrived:
            arrived.add(offset % RING)
            sib_copy(offset).wait_recv()

    for hop in range(1, 5):
        for direction, half in lanes:
            last = hops(direction, half)
            if hop <= last:
                offset = direction * (last - hop + 1)
                have(offset)
                number = hop_number(direction, half, hop)
                value = mine(wrap(z + offset, RING), half)
                if hop > 1:
                    hop_copy(direction, half, hop - 1).wait_recv()
                    value = value + in_buf[number - 1].astype(jnp.float32)
                out_buf[number] = value.astype(jnp.bfloat16)
                hop_copy(direction, half, hop).start()
    have(0)
    for half in range(2):
        value = mine(z, half)
        for direction in (1, -1):
            last = hops(direction, half)
            hop_copy(direction, half, last).wait_recv()
            value = value + in_buf[hop_number(direction, half, last)].astype(jnp.float32)
        total[:, half * HALF : (half + 1) * HALF] = value
    for offset in order:
        sib_copy(offset).wait_send()
    for direction, half in lanes:
        for hop in range(1, hops(direction, half) + 1):
            hop_copy(direction, half, hop).wait_send()


def normalize(widened, gain):
    scale = lax.rsqrt(jnp.mean(widened * widened, axis=-1, keepdims=True) + 1e-06)
    return (widened * scale * gain).astype(jnp.bfloat16)


def live_lanes(counts):
    row = lax.broadcasted_iota(jnp.int32, (SHARD, 16), 0)
    first = lax.broadcasted_iota(jnp.int32, (SHARD, 16), 1) * SLOTS
    spread = jnp.where((row >= first) & (row < first + SLOTS), 1.0, 0.0).astype(jnp.bfloat16)
    block = lax.broadcasted_iota(jnp.int32, (16, 128), 0).astype(jnp.float32)
    count_of = jnp.dot(spread, counts.astype(jnp.bfloat16), preferred_element_type=jnp.float32)
    block_of = jnp.dot(spread, block.astype(jnp.bfloat16), preferred_element_type=jnp.float32)
    slot = lax.broadcasted_iota(jnp.int32, (SHARD, 128), 0).astype(jnp.float32) - block_of * SLOTS
    return jnp.where(slot < count_of, 1.0, 0.0)


ORDER = [
    (0, 0), (1, 0), (-1, 0), (0, 1), (0, -1), (1, 1), (1, -1), (-1, 1), (-1, -1), (2, 0), (0, 2),
    (2, 1), (2, -1), (1, 2), (-1, 2), (2, 2),
]


def offset_slot(dx, dy):
    return ORDER.index((((dx + 1) % SIDE) - 1, ((dy + 1) % SIDE) - 1))


def torus_place():
    place = lax.axis_index("seq")
    return lax.div(place, SIDE), lax.rem(place, SIDE)


def at_torus(px, py):
    return {"seq": wrap(px, SIDE) * SIDE + wrap(py, SIDE)}


class TorusGather:
    def __init__(self, block, send, recv):
        self.block, self.send, self.recv = block, send, recv
        self.x, self.y = torus_place()

    def copy(self, quarter, number):
        d = 1 if quarter % 2 == 0 else -1
        line, kind = (0, number) if number < 3 else divmod(number - 3, 3)
        step = -d if kind == 1 else d
        along = [-d, d, -2 * d][kind]
        if number < 3:
            origin, move = (along, 0), (step, 0)
        else:
            origin, move = ([0, -d, d, -2 * d][line], along), (0, step)
        source = (origin[0] + move[0], origin[1] + move[1])
        if quarter < 2:
            origin, move, source = origin[::-1], move[::-1], source[::-1]
        place = quarter * 15 + number
        return remote(
            self.block(offset_slot(*source), quarter), self.block(offset_slot(*origin), quarter),
            self.send.at[place], self.recv.at[place], at_torus(self.x + move[0], self.y + move[1]),
        )

    def start(self, quarter, *numbers):
        for number in numbers:
            self.copy(quarter, number).start()

    def arrive(self, *numbers):
        for number in numbers:
            for quarter in range(4):
                self.copy(quarter, number).wait_recv()

    def stage(self, stage):
        for quarter in range(4):
            for needed, following in [
                [(None, (0, 1, 3, 4))],
                [(0, (2, 6, 7)), (1, (9, 10)), (3, (5,))],
                [(2, (12, 13)), (6, (8,)), (9, (11,))],
                [(12, (14,))],
            ][stage]:
                if needed is not None:
                    self.copy(quarter, needed).wait_recv()
                self.start(quarter, *following)

    def finish(self):
        for quarter in range(4):
            for number in range(15):
                self.copy(quarter, number).wait_send()


def block_kernel(
    tokens, rows, counts, ids, gains, w_query, w_keyval, w_out, router, w_expert,
    picked, total,
    gathered, kv, tallies, acc, weights, part, sib, out_buf, in_buf, head, normed, routed, hidden, result,
    sib2, out_buf2, in_buf2,
    g_send, g_recv, gs_send, gs_recv, kv_send, kv_recv, count_send, count_recv, w_send, w_recv,
    r_send, r_recv, rs_send, rs_recv, n_send, n_recv, ns_send, ns_recv, b_send, b_recv, bs_send, bs_recv,
):
    f32, bf16 = jnp.float32, jnp.bfloat16
    place = lax.axis_index("exp")
    seq = lax.axis_index("seq")
    x, y = torus_place()
    greet(
        ring_partners()
        + [at_torus(x + dx, y + dy) for dx, dy in ((0, 1), (0, -1), (0, 2), (1, 0), (-1, 0), (2, 0))]
    )

    weights[0] = w_expert[...]
    w_gather = TorusGather(lambda slot, quarter: weights.at[slot, :, :, pl.ds(quarter * 512, 512)], w_send, w_recv)
    w_gather.stage(0)

    row16 = lax.broadcasted_iota(jnp.int32, (16, 128), 0)
    tally = jnp.zeros((16, 128), f32)
    for device in range(16):
        tally = jnp.where(row16 == device, counts[device].astype(f32), tally)
    tallies[x, y] = tally

    def count_copy(axis, shift):
        number = (0 if axis == 1 else 3) + shift - 1
        if axis == 1:
            ref, target = tallies.at[x, y], at_torus(x, y + shift)
        else:
            ref, target = tallies.at[x], at_torus(x + shift, y)
        return remote(ref, ref, count_send.at[number], count_recv.at[number], target)

    def count_arrival(axis, shift):
        number = (0 if axis == 1 else 3) + shift - 1
        if axis == 1:
            ref, target = tallies.at[x, wrap(y - shift, SIDE)], at_torus(x, y + shift)
        else:
            ref, target = tallies.at[wrap(x - shift, SIDE)], at_torus(x + shift, y)
        return remote(ref, ref, count_send.at[number], count_recv.at[number], target)

    for shift in (1, 2, 3):
        count_copy(1, shift).start()

    mine = rows[pl.ds(place, 1), :]
    onehot = jnp.where(
        lax.broadcasted_iota(jnp.int32, (tokens.shape[0], SLOTS), 0) == mine, 1.0, 0.0
    ).T.astype(bf16)
    chosen = jnp.dot(onehot, tokens[...], preferred_element_type=f32)
    picked[...] = chosen.astype(bf16)
    gathered[place] = normalize(chosen, gains[0:1, :])
    ring_gather(gathered, g_send, g_recv, gs_send, gs_recv)
    for shift in (1, 2, 3):
        count_arrival(1, shift).wait_recv()
    for shift in (1, 2, 3):
        count_copy(0, shift).start()

    inputs = gathered[...].reshape(SHARD, WIDTH)
    keys = jnp.dot(inputs, w_keyval[0], preferred_element_type=f32).astype(bf16)
    values = jnp.dot(inputs, w_keyval[1], preferred_element_type=f32)
    values = (values * live_lanes(tally)).astype(bf16)
    kv[0, :, :, 0:HEAD_DIM] = keys.reshape(4, QUARTER, HEAD_DIM)
    kv[0, :, :, HEAD_DIM:] = values.reshape(4, QUARTER, HEAD_DIM)
    kv_gather = TorusGather(lambda slot, quarter: kv.at[slot, quarter], kv_send, kv_recv)
    kv_gather.stage(0)
    queries = jnp.dot(inputs, w_query[...], preferred_element_type=f32).astype(bf16)

    c1 = HEAD_DIM ** (-0.5) / softcap_limit
    c2 = softcap_limit * math.log2(math.e)
    tile = 256

    def unit(dx, dy):
        diagonal = dx == 0 and dy == 0
        slot = offset_slot(dx, dy)
        unit_keys = kv[slot, :, :, 0:HEAD_DIM].reshape(SHARD, HEAD_DIM)
        live = live_lanes(tallies[wrap(x + dx, SIDE), wrap(y + dy, SIDE)]).astype(bf16)
        unit_values = jnp.concatenate([kv[slot, :, :, HEAD_DIM:].reshape(SHARD, HEAD_DIM), live], axis=1)

        @pl.loop(0, SHARD // tile)
        def _(number):
            first = pl.multiple_of(number * tile, tile)
            scores = lax.dot_general(
                query_ref[pl.ds(first, tile), :], unit_keys, (((1,), (1,)), ((), ())), preferred_element_type=f32
            )
            weight = jnp.exp2(c2 * jnp.tanh(scores * c1))
            if diagonal:
                row = lax.broadcasted_iota(jnp.int32, (tile, SHARD), 0) + first
                column = lax.broadcasted_iota(jnp.int32, (tile, SHARD), 1)
                weight = jnp.where(column <= row, weight, 0.0)
            term = jnp.dot(weight.astype(bf16), unit_values, preferred_element_type=f32)
            if diagonal:
                acc[pl.ds(first, tile), :] = term
            else:
                acc[pl.ds(first, tile), :] += term

    query_ref = hidden.at[0, :, :]
    query_ref[...] = queries

    def earlier(*offsets):
        for dx, dy in offsets:
            px, py = wrap(x + dx, SIDE), wrap(y + dy, SIDE)

            @pl.when(px * SIDE + py < seq)
            def _():
                unit(dx, dy)

    unit(0, 0)
    kv_gather.stage(1)
    kv_gather.arrive(4)
    for shift in (1, 2, 3):
        count_arrival(0, shift).wait_recv()
    earlier((1, 0), (-1, 0))
    kv_gather.stage(2)
    w_gather.stage(1)
    earlier((0, 1), (0, -1))
    kv_gather.stage(3)
    kv_gather.arrive(7, 10, 5)
    earlier((1, 1), (1, -1), (-1, 1), (-1, -1), (2, 0), (0, 2))
    kv_gather.arrive(13, 8, 11)
    earlier((2, 1), (2, -1), (1, 2), (-1, 2))
    kv_gather.arrive(14)
    earlier((2, 2))

    mass = acc[:, HEAD_DIM:]
    query_ref[...] = (acc[:, 0:HEAD_DIM] / jnp.where(mass > 0, mass, 1.0)).astype(bf16)

    @pl.loop(0, 4)
    def _(number):
        block = query_ref[pl.ds(pl.multiple_of(number * 4 * SLOTS, 4 * SLOTS), 4 * SLOTS), :]
        sums = jnp.dot(block, w_out[...], preferred_element_type=f32).astype(bf16)
        part[pl.ds(number * 4, 4)] = sums.reshape(4, SLOTS, WIDTH)

    ring_scatter(part, sib, out_buf, in_buf, head, r_send, r_recv, rs_send, rs_recv)
    w_gather.stage(2)
    normed[place] = normalize(picked[...].astype(f32) + head[...], gains[1:2, :])
    ring_gather(normed, n_send, n_recv, ns_send, ns_recv)
    w_gather.stage(3)

    named_by = jnp.concatenate(
        [
            jnp.max(jnp.where(ids[...] == expert, 1.0, 0.0), axis=0, keepdims=True)
            for expert in range(16)
        ],
        axis=0,
    )
    named = jnp.max(jnp.where(ids[...] == place, 1.0, 0.0), axis=0, keepdims=True)
    before = jnp.where(
        lax.broadcasted_iota(jnp.int32, (SHARD, SHARD), 0) <= lax.broadcasted_iota(jnp.int32, (SHARD, SHARD), 1), 1.0, 0.0
    ).astype(bf16)
    named8 = jnp.broadcast_to(named, (16, SHARD))
    rank = jnp.dot(named8.astype(bf16), before, preferred_element_type=f32) * named8
    rank_column = rank.T[:, 0:1]
    capacity = routed.shape[0]
    select = jnp.where(
        lax.broadcasted_iota(jnp.int32, (capacity, SHARD), 0).astype(f32) + 1.0 == rank[0:1, :], 1.0, 0.0
    ).astype(bf16)
    spread = jnp.where(
        lax.broadcasted_iota(jnp.int32, (SHARD, capacity), 1).astype(f32) + 1.0 == rank_column, 1.0, 0.0
    ).astype(bf16)
    everyone = normed[...].reshape(SHARD, WIDTH)
    routed[...] = jnp.dot(select, everyone, preferred_element_type=f32).astype(bf16)
    scores = lax.dot_general(everyone, router[...], (((1,), (1,)), ((), ())), preferred_element_type=f32)
    scores = named_by.T / (1.0 + jnp.exp(-scores))
    own = jnp.where(lax.broadcasted_iota(jnp.int32, (SHARD, 16), 1) == place, scores, 0.0)
    share = jnp.sum(own, axis=1, keepdims=True) / jnp.sum(scores, axis=1, keepdims=True)

    def experts(first, count):
        @pl.loop(0, count)
        def _(number):
            slot = first + number
            gated = lax.dot_general(
                routed[...], weights[slot, 0], (((1,), (1,)), ((), ())), preferred_element_type=f32
            )
            upward = lax.dot_general(
                routed[...], weights[slot, 1], (((1,), (1,)), ((), ())), preferred_element_type=f32
            )
            units = (gated / (1.0 + jnp.exp(-gated)) * upward).astype(bf16)
            for column in range(4):
                columns = slice(column * 512, column * 512 + 512)
                term = jnp.dot(units, weights[slot, 2, :, columns], preferred_element_type=f32)
                result[:, columns] += term

    result[...] = jnp.zeros_like(result)
    w_gather.arrive(4)
    experts(0, 5)
    w_gather.arrive(7, 10, 5)
    experts(5, 6)
    w_gather.arrive(13, 8, 11)
    experts(11, 4)
    w_gather.arrive(14)
    experts(15, 1)

    for column in range(4):
        columns = slice(column * 512, column * 512 + 512)
        term = jnp.dot(spread, result[:, columns].astype(bf16), preferred_element_type=f32) * share
        part[:, :, columns] = term.astype(bf16).reshape(16, SLOTS, 512)
    ring_scatter(part, sib2, out_buf2, in_buf2, total, b_send, b_recv, bs_send, bs_recv)
    total[...] += head[...]

    for shift in (1, 2, 3):
        count_copy(1, shift).wait_send()
        count_copy(0, shift).wait_send()
    kv_gather.finish()
    w_gather.finish()


def finish_kernel(tokens, rows, counts, picked, total, depth_router, mixed, delta):
    f32, bf16 = jnp.float32, jnp.bfloat16
    place = lax.axis_index("exp")
    live = lax.broadcasted_iota(jnp.int32, (SLOTS, 128), 0) < counts[place]
    live = jnp.where(live, 1.0, 0.0)[:, 0:1] > 0
    change = jnp.where(live, total[...], 0.0)
    delta[...] = change
    logit = jnp.sum(picked[...].astype(f32) * depth_router[...].astype(f32), axis=1, keepdims=True)
    update = change / (1.0 + jnp.exp(-logit))
    high = update.astype(bf16)
    low = (update - high.astype(f32)).astype(bf16)
    onehot = jnp.where(
        lax.broadcasted_iota(jnp.int32, (tokens.shape[0], SLOTS), 0) == rows[pl.ds(place, 1), :], 1.0, 0.0
    ).astype(bf16)
    added = jnp.dot(onehot, high, preferred_element_type=f32) + jnp.dot(onehot, low, preferred_element_type=f32)
    mixed[...] = (tokens[...].astype(f32) + added).astype(bf16)


def dma(count):
    return pltpu.SemaphoreType.DMA((count,))


GATHER_SEMS = [dma(16), dma(16), dma(17), dma(17)]
SCATTER_BUFS = [
    pltpu.VMEM((RING, SLOTS, WIDTH), jnp.bfloat16),
    pltpu.VMEM((16, SLOTS, HALF), jnp.bfloat16),
    pltpu.VMEM((16, SLOTS, HALF), jnp.bfloat16),
]
SCATTER_SEMS = [dma(16), dma(16), dma(8), dma(8)]
SMEM = pl.BlockSpec(memory_space=pltpu.SMEM)
CAPACITY = 416


def local(
    tokens, pick_rows, pick_counts, expert_ids, norm_gains, depth_router,
    w_query, w_keyval, w_out, expert_router, w_expert,
):
    f32, bf16 = jnp.float32, jnp.bfloat16
    units = w_expert.shape[3]
    picked, total = pl.pallas_call(
        block_kernel,
        out_shape=(
            jax.ShapeDtypeStruct((SLOTS, WIDTH), bf16),
            jax.ShapeDtypeStruct((SLOTS, WIDTH), f32),
        ),
        in_specs=[VMEM, VMEM, SMEM] + [VMEM] * 7,
        out_specs=(VMEM,) * 2,
        scratch_shapes=[
            pltpu.VMEM((16, SLOTS, WIDTH), bf16),
            pltpu.VMEM((16, 4, QUARTER, 2 * HEAD_DIM), bf16),
            pltpu.VMEM((SIDE, SIDE, 16, 128), f32),
            pltpu.VMEM((SHARD, 2 * HEAD_DIM), f32),
            pltpu.VMEM((16, 3, units, WIDTH), bf16),
            pltpu.VMEM((16, SLOTS, WIDTH), bf16),
        ]
        + SCATTER_BUFS
        + [
            pltpu.VMEM((SLOTS, WIDTH), f32),
            pltpu.VMEM((16, SLOTS, WIDTH), bf16),
            pltpu.VMEM((CAPACITY, WIDTH), bf16),
            pltpu.VMEM((1, SHARD, HEAD_DIM), bf16),
            pltpu.VMEM((CAPACITY, WIDTH), f32),
        ]
        + SCATTER_BUFS
        + GATHER_SEMS
        + [dma(60), dma(60), dma(6), dma(6), dma(60), dma(60)]
        + SCATTER_SEMS
        + GATHER_SEMS
        + SCATTER_SEMS,
        compiler_params=pltpu.CompilerParams(collective_id=0, has_side_effects=True, vmem_limit_bytes=60 << 20),
        name="block",
    )(
        tokens, pick_rows, pick_counts, expert_ids.T, norm_gains, w_query, w_keyval, w_out,
        expert_router.T, jnp.transpose(w_expert[0], (0, 2, 1)),
    )
    return pl.pallas_call(
        finish_kernel,
        out_shape=(
            jax.ShapeDtypeStruct(tokens.shape, bf16),
            jax.ShapeDtypeStruct((SLOTS, WIDTH), f32),
        ),
        in_specs=[VMEM, VMEM, SMEM] + [VMEM] * 3,
        out_specs=(VMEM,) * 2,
        compiler_params=pltpu.CompilerParams(vmem_limit_bytes=32 << 20),
        name="finish",
    )(tokens, pick_rows, pick_counts, picked, total, depth_router[None, :])


def solution(mesh):
    in_specs = (
        P(("seq", "exp"), None), P("seq", None), P("seq"), P("seq", None), P(), P(),
        P(None, "exp"), P(None, None, "exp"), P("exp", None), P(), P("exp", None, None, "seq"),
    )
    out_specs = (P(("seq", "exp"), None), P(("seq", "exp"), None))
    return jax.shard_map(local, mesh=mesh, in_specs=in_specs, out_specs=out_specs, check_vma=False)
```

```python
import functools
import math

import jax
import jax.numpy as jnp
from jax import lax
from jax.experimental import pallas as pl
from jax.experimental.pallas import tpu as pltpu
from jax.sharding import PartitionSpec as P

HEAD_DIM = 128
softcap_limit = 20.0
MESH = pl.DeviceIdType.MESH
SIDE = 4
RING = 8
SLOTS = 48
SHARD = 768
WIDTH = 2048
HALF = 1024
QUARTER = 192
VMEM = pl.BlockSpec(memory_space=pltpu.VMEM)


def wrap(value, size):
    return lax.rem(value + size, size)


def hops(direction, half):
    return 4 if (direction > 0) == (half == 0) else 3


def hop_number(direction, half, hop):
    return ((0 if direction > 0 else 1) * 2 + half) * 4 + hop - 1


def at_exp(index):
    return {"exp": index}


def ring_place():
    place = lax.axis_index("exp")
    return lax.div(place, 2), lax.rem(place, 2)


def greet(partners):
    barrier = pltpu.get_barrier_semaphore()
    for partner in partners:
        pl.semaphore_signal(barrier, inc=1, device_id=partner, device_id_type=MESH)
    pl.semaphore_wait(barrier, len(partners))


def ring_partners():
    z, core = ring_place()
    return [
        at_exp(2 * wrap(z + 1, RING) + core),
        at_exp(2 * wrap(z - 1, RING) + core),
        at_exp(2 * z + 1 - core),
    ]


def remote(src, dst, send, recv, target):
    return pltpu.make_async_remote_copy(
        src_ref=src, dst_ref=dst, send_sem=send, recv_sem=recv, device_id=target, device_id_type=MESH
    )


def ring_gather(buf, send, recv, sib_send, sib_recv, between=lambda hop: None):
    z, core = ring_place()
    sibling = at_exp(2 * z + 1 - core)

    def part(origin, side, half):
        return buf.at[2 * origin + side, :, pl.ds(half * HALF, HALF)]

    def hop_copy(direction, half, hop, arriving):
        origin = wrap(z - direction * (hop if arriving else hop - 1), RING)
        ref = part(origin, core, half)
        number = hop_number(direction, half, hop)
        return remote(ref, ref, send.at[number], recv.at[number], at_exp(2 * wrap(z + direction, RING) + core))

    def sib_copy(direction, half, hop, arriving):
        origin = wrap(z - direction * hop, RING)
        ref = part(origin, 1 - core if arriving else core, half)
        number = hop_number(direction, half, hop)
        return remote(ref, ref, sib_send.at[number], sib_recv.at[number], sibling)

    def own_copy(arriving):
        ref = buf.at[2 * z + (1 - core if arriving else core)]
        return remote(ref, ref, sib_send.at[16], sib_recv.at[16], sibling)

    lanes = [(1, 0), (-1, 1), (1, 1), (-1, 0)]
    for direction, half in lanes:
        hop_copy(direction, half, 1, False).start()
    own_copy(False).start()
    for hop in range(1, 5):
        for direction, half in lanes:
            if hop <= hops(direction, half):
                hop_copy(direction, half, hop, True).wait_recv()
                if hop < hops(direction, half):
                    hop_copy(direction, half, hop + 1, False).start()
                sib_copy(direction, half, hop, False).start()
        between(hop)
    own_copy(True).wait_recv()
    own_copy(False).wait_send()
    for hop in range(1, 5):
        for direction, half in lanes:
            if hop <= hops(direction, half):
                sib_copy(direction, half, hop, True).wait_recv()
                sib_copy(direction, half, hop, False).wait_send()
                hop_copy(direction, half, hop, False).wait_send()


def ring_scatter(part, sib, out_buf, in_buf, total, send, recv, sib_send, sib_recv, between=lambda hop: None):
    z, core = ring_place()
    sibling = at_exp(2 * z + 1 - core)

    def sib_copy(offset):
        target = wrap(z + offset, RING)
        return remote(
            part.at[2 * target + 1 - core], sib.at[target], sib_send.at[offset % RING], sib_recv.at[offset % RING], sibling
        )

    def mine(target, half):
        columns = pl.ds(half * HALF, HALF)
        return part[2 * target + core, :, columns].astype(jnp.float32) + sib[target, :, columns].astype(jnp.float32)

    def hop_copy(direction, half, hop):
        number = hop_number(direction, half, hop)
        return remote(
            out_buf.at[number], in_buf.at[number], send.at[number], recv.at[number],
            at_exp(2 * wrap(z + direction, RING) + core),
        )

    order = [4, 3, -3, 2, -2, 1, -1, 0]
    for offset in order:
        sib_copy(offset).start()
    arrived = set()
    lanes = [(1, 0), (-1, 1), (1, 1), (-1, 0)]

    def have(offset):
        if offset % RING not in arrived:
            arrived.add(offset % RING)
            sib_copy(offset).wait_recv()

    for hop in range(1, 5):
        for direction, half in lanes:
            last = hops(direction, half)
            if hop <= last:
                offset = direction * (last - hop + 1)
                have(offset)
                number = hop_number(direction, half, hop)
                value = mine(wrap(z + offset, RING), half)
                if hop > 1:
                    hop_copy(direction, half, hop - 1).wait_recv()
                    value = value + in_buf[number - 1].astype(jnp.float32)
                out_buf[number] = value.astype(jnp.bfloat16)
                hop_copy(direction, half, hop).start()
        between(hop)
    have(0)
    for half in range(2):
        value = mine(z, half)
        for direction in (1, -1):
            last = hops(direction, half)
            hop_copy(direction, half, last).wait_recv()
            value = value + in_buf[hop_number(direction, half, last)].astype(jnp.float32)
        total[:, half * HALF : (half + 1) * HALF] = value
    for offset in order:
        sib_copy(offset).wait_send()
    for direction, half in lanes:
        for hop in range(1, hops(direction, half) + 1):
            hop_copy(direction, half, hop).wait_send()


def normalize(widened, gain):
    scale = lax.rsqrt(jnp.mean(widened * widened, axis=-1, keepdims=True) + 1e-06)
    return (widened * scale * gain).astype(jnp.bfloat16)


def live_lanes(counts):
    row = lax.broadcasted_iota(jnp.int32, (SHARD, 16), 0)
    first = lax.broadcasted_iota(jnp.int32, (SHARD, 16), 1) * SLOTS
    spread = jnp.where((row >= first) & (row < first + SLOTS), 1.0, 0.0).astype(jnp.bfloat16)
    block = lax.broadcasted_iota(jnp.int32, (16, 128), 0).astype(jnp.float32)
    count_of = jnp.dot(spread, counts.astype(jnp.bfloat16), preferred_element_type=jnp.float32)
    block_of = jnp.dot(spread, block.astype(jnp.bfloat16), preferred_element_type=jnp.float32)
    slot = lax.broadcasted_iota(jnp.int32, (SHARD, 128), 0).astype(jnp.float32) - block_of * SLOTS
    return jnp.where(slot < count_of, 1.0, 0.0)


ORDER = [
    (0, 0), (1, 0), (-1, 0), (0, 1), (0, -1), (1, 1), (1, -1), (-1, 1), (-1, -1), (2, 0), (0, 2),
    (2, 1), (2, -1), (1, 2), (-1, 2), (2, 2),
]


def offset_slot(dx, dy):
    return ORDER.index((((dx + 1) % SIDE) - 1, ((dy + 1) % SIDE) - 1))


def torus_place():
    place = lax.axis_index("seq")
    return lax.div(place, SIDE), lax.rem(place, SIDE)


def at_torus(px, py):
    return {"seq": wrap(px, SIDE) * SIDE + wrap(py, SIDE)}


def along(axis, step):
    x, y = torus_place()
    return at_torus(x + step, y) if axis == 0 else at_torus(x, y + step)


class TorusGather:
    def __init__(self, block, send, recv):
        self.block, self.send, self.recv = block, send, recv
        self.x, self.y = torus_place()

    def copy(self, quarter, number):
        d = 1 if quarter % 2 == 0 else -1
        line, kind = (0, number) if number < 3 else divmod(number - 3, 3)
        step = -d if kind == 1 else d
        along = [-d, d, -2 * d][kind]
        if number < 3:
            origin, move = (along, 0), (step, 0)
        else:
            origin, move = ([0, -d, d, -2 * d][line], along), (0, step)
        source = (origin[0] + move[0], origin[1] + move[1])
        if quarter < 2:
            origin, move, source = origin[::-1], move[::-1], source[::-1]
        place = quarter * 15 + number
        return remote(
            self.block(offset_slot(*source), quarter), self.block(offset_slot(*origin), quarter),
            self.send.at[place], self.recv.at[place], at_torus(self.x + move[0], self.y + move[1]),
        )

    def start(self, quarter, *numbers):
        for number in numbers:
            self.copy(quarter, number).start()

    def arrive(self, *numbers):
        for number in numbers:
            for quarter in range(4):
                self.copy(quarter, number).wait_recv()

    def stage(self, stage, quarters=range(4)):
        for quarter in quarters:
            for needed, following in [
                [(None, (0, 1, 3, 4))],
                [(0, (2, 6, 7)), (1, (9, 10)), (3, (5,))],
                [(2, (12, 13)), (6, (8,)), (9, (11,))],
                [(12, (14,))],
            ][stage]:
                if needed is not None:
                    self.copy(quarter, needed).wait_recv()
                self.start(quarter, *following)

    def finish(self):
        for quarter in range(4):
            for number in range(15):
                self.copy(quarter, number).wait_send()


class LineGather:
    def __init__(self, axis, block, send, recv):
        self.axis, self.block, self.send, self.recv = axis, block, send, recv

    def copy(self, half, number):
        d = 1 if half == 0 else -1
        step = -d if number == 1 else d
        origin = [-d, d, -2 * d][number]
        place = half * 3 + number
        return remote(
            self.block((origin + step) % SIDE, half), self.block(origin % SIDE, half),
            self.send.at[place], self.recv.at[place], along(self.axis, step),
        )

    def begin(self):
        for half in range(2):
            self.copy(half, 0).start()
            self.copy(half, 1).start()

    def forward(self):
        for half in range(2):
            self.copy(half, 0).wait_recv()
            self.copy(half, 2).start()
        for half in range(2):
            self.copy(half, 1).wait_recv()

    def last(self):
        for half in range(2):
            self.copy(half, 2).wait_recv()

    def finish(self):
        for half in range(2):
            for number in range(3):
                self.copy(half, number).wait_send()


def block_kernel(
    tokens, rows, counts, ids, gains, depth_router, w_query_hbm, w_keyval_hbm, w_out_hbm, router, w_expert,
    mixed, delta,
    w_query, w_keyval, w_out, picked, total, gathered, kv, query, tallies, acc, term_out, term_in, mass_out, mass_in,
    attended, weights, part, sib, out_buf, in_buf, head, normed, routed, units_of, result,
    sib2, out_buf2, in_buf2,
    local_sem, g_send, g_recv, gs_send, gs_recv, kv_send, kv_recv, q_send, q_recv, t_send, t_recv, m_send, m_recv,
    count_send, count_recv, w_send, w_recv,
    r_send, r_recv, rs_send, rs_recv, n_send, n_recv, ns_send, ns_recv, b_send, b_recv, bs_send, bs_recv,
):
    f32, bf16 = jnp.float32, jnp.bfloat16
    place = lax.axis_index("exp")
    seq = lax.axis_index("seq")
    w_units = w_expert.shape[1]
    x, y = torus_place()
    loads = [
        pltpu.make_async_copy(source, target, local_sem.at[number])
        for number, (source, target) in enumerate(
            ((w_keyval_hbm, w_keyval), (w_query_hbm, w_query), (w_out_hbm, w_out))
        )
    ]
    for load in loads:
        load.start()
    weights[0, 0 : w_units] = w_expert[0]
    weights[0, w_units : 2 * w_units] = w_expert[1]
    weights[0, 2 * w_units :] = jnp.zeros_like(weights[0, 2 * w_units :])
    weights[0, 2 * w_units : 3 * w_units] = w_expert[2]
    greet(
        ring_partners()
        + [at_torus(x + dx, y + dy) for dx, dy in ((0, 1), (0, -1), (0, 2), (1, 0), (-1, 0))]
    )

    w_gather = TorusGather(lambda slot, quarter: weights.at[slot, :, pl.ds(quarter * 512, 512)], w_send, w_recv)
    w_gather.stage(0)

    row16 = lax.broadcasted_iota(jnp.int32, (16, 128), 0)
    tally = jnp.zeros((16, 128), f32)
    for device in range(16):
        tally = jnp.where(row16 == device, counts[device].astype(f32), tally)
    tallies[0] = tally

    def count_copy(shift):
        return remote(
            tallies.at[0], tallies.at[SIDE - shift], count_send.at[shift - 1], count_recv.at[shift - 1],
            at_torus(x, y + shift),
        )

    for shift in (1, 2, 3):
        count_copy(shift).start()
    acc[...] = jnp.zeros_like(acc)
    units_of[...] = jnp.zeros_like(units_of)

    mine = rows[pl.ds(place, 1), :]
    onehot = jnp.where(
        lax.broadcasted_iota(jnp.int32, (tokens.shape[0], SLOTS), 0) == mine, 1.0, 0.0
    ).T.astype(bf16)
    chosen = jnp.dot(onehot, tokens[...], preferred_element_type=f32)
    picked[...] = chosen.astype(bf16)
    gathered[place] = normalize(chosen, gains[0:1, :])
    ring_gather(gathered, g_send, g_recv, gs_send, gs_recv)
    for load in loads:
        load.wait()
    half_rows = SHARD // 2
    inputs = gathered[...].reshape(SHARD, WIDTH)
    keys = jnp.dot(inputs, w_keyval[0], preferred_element_type=f32).astype(bf16)
    values = jnp.dot(inputs, w_keyval[1], preferred_element_type=f32)
    values = (values * live_lanes(tally)).astype(bf16)
    kv[0, :, :, 0:HEAD_DIM] = keys.reshape(2, half_rows, HEAD_DIM)
    kv[0, :, :, HEAD_DIM:] = values.reshape(2, half_rows, HEAD_DIM)
    kv_gather = LineGather(1, lambda offset, half: kv.at[offset, half], kv_send, kv_recv)
    kv_gather.begin()
    queries = jnp.dot(inputs, w_query[...], preferred_element_type=f32).astype(bf16)
    query[0] = queries.reshape(2, half_rows, HEAD_DIM)
    q_gather = LineGather(0, lambda offset, half: query.at[offset, half], q_send, q_recv)
    q_gather.begin()

    c1 = HEAD_DIM ** (-0.5) / softcap_limit
    c2 = softcap_limit * math.log2(math.e)
    tile = 384

    def unit(dx, dy, diagonal=False):
        unit_keys = kv[dy, :, :, 0:HEAD_DIM].reshape(SHARD, HEAD_DIM)
        live = live_lanes(tallies[dy]).astype(bf16)
        unit_values = jnp.concatenate([kv[dy, :, :, HEAD_DIM:].reshape(SHARD, HEAD_DIM), live], axis=1)

        for half in range(2):

            @pl.loop(0, half_rows // tile)
            def _(number):
                first = pl.multiple_of(number * tile, tile)
                scores = lax.dot_general(
                    query[dx, half, pl.ds(first, tile), :], unit_keys, (((1,), (1,)), ((), ())),
                    preferred_element_type=f32,
                )
                weight = jnp.exp2(c2 * jnp.tanh(scores * c1))
                if diagonal:
                    row = lax.broadcasted_iota(jnp.int32, (tile, SHARD), 0) + first + half * half_rows
                    column = lax.broadcasted_iota(jnp.int32, (tile, SHARD), 1)
                    weight = jnp.where(column <= row, weight, 0.0)
                acc[dx, half, pl.ds(first, tile), :] += jnp.dot(
                    weight.astype(bf16), unit_values, preferred_element_type=f32
                )

    def earlier(dx, dy):
        @pl.when((wrap(x + dx, SIDE) > x) if dx else (wrap(y + dy, SIDE) < y))
        def _():
            unit(dx, dy)

    unit(0, 0, True)
    q_gather.forward()
    kv_gather.forward()
    earlier(1, 0)
    earlier(3, 0)
    for shift in (1, 2, 3):
        count_copy(shift).wait_recv()
    q_gather.last()
    w_gather.stage(1, (0,))
    earlier(2, 0)
    for dy in (1, 3):
        for dx in (2, 1, 3, 0):
            earlier(dx, dy)
    kv_gather.last()
    earlier(2, 2)

    def term_copies(direction, half, hop):
        number = (0 if direction > 0 else 3) + (hop if half == (0 if direction > 0 else 1) else 2)
        target = along(0, direction)
        return (
            remote(term_out.at[number], term_in.at[number], t_send.at[number], t_recv.at[number], target),
            remote(mass_out.at[number], mass_in.at[number], m_send.at[number], m_recv.at[number], target),
        ), number

    def send_terms(direction, half, hop, dx, received):
        copies, number = term_copies(direction, half, hop)
        value = acc[dx, half, :, 0:HEAD_DIM]
        mass = acc[dx, half, :, HEAD_DIM:].T[0:8, :]
        if received is not None:
            value = value + term_in[received].astype(f32)
            mass = mass + mass_in[received]
        term_out[number] = value.astype(bf16)
        mass_out[number] = mass
        for copy in copies:
            copy.start()

    def take_terms(direction, half, hop):
        copies, number = term_copies(direction, half, hop)
        for copy in copies:
            copy.wait_recv()
        return number

    send_terms(1, 0, 0, 2, None)
    send_terms(-1, 1, 0, 2, None)
    earlier(1, 2)
    earlier(3, 2)
    send_terms(1, 1, 0, 1, None)
    send_terms(-1, 0, 0, 3, None)
    send_terms(1, 0, 1, 1, take_terms(1, 0, 0))
    send_terms(-1, 1, 1, 3, take_terms(-1, 1, 0))
    w_gather.stage(1, (1,))
    earlier(0, 2)
    for half in range(2):
        value = acc[0, half, :, 0:HEAD_DIM]
        mass = acc[0, half, :, HEAD_DIM:]
        for direction in (-1, 1):
            number = take_terms(direction, half, 1 if half == (0 if direction > 0 else 1) else 0)
            value = value + term_in[number].astype(f32)
            mass = mass + jnp.broadcast_to(mass_in[number].T[:, 0:1], mass.shape)
        attended[half * half_rows : (half + 1) * half_rows, :] = (
            value / jnp.where(mass > 0, mass, 1.0)
        ).astype(bf16)

    @pl.loop(0, 4)
    def _(number):
        block = attended[pl.ds(pl.multiple_of(number * 4 * SLOTS, 4 * SLOTS), 4 * SLOTS), :]
        sums = jnp.dot(block, w_out[...], preferred_element_type=f32).astype(bf16)
        part[pl.ds(number * 4, 4)] = sums.reshape(4, SLOTS, WIDTH)

    def during_scatter(hop):
        if hop == 1:
            w_gather.stage(1, (2,))
        if hop == 2:
            w_gather.stage(1, (3,))
        if hop == 3:
            w_gather.stage(2, (0,))
        if hop == 4:
            w_gather.stage(2, (1,))

    def during_gather(hop):
        if hop == 2:
            w_gather.stage(2, (2,))
        if hop == 3:
            w_gather.stage(2, (3,))
        if hop == 4:
            w_gather.stage(3)

    ring_scatter(part, sib, out_buf, in_buf, head, r_send, r_recv, rs_send, rs_recv, during_scatter)
    normed[place] = normalize(picked[...].astype(f32) + head[...], gains[1:2, :])
    ring_gather(normed, n_send, n_recv, ns_send, ns_recv, during_gather)

    named_by = jnp.concatenate(
        [
            jnp.max(jnp.where(ids[...] == expert, 1.0, 0.0), axis=0, keepdims=True)
            for expert in range(16)
        ],
        axis=0,
    )
    named = jnp.max(jnp.where(ids[...] == place, 1.0, 0.0), axis=0, keepdims=True)
    before = jnp.where(
        lax.broadcasted_iota(jnp.int32, (SHARD, SHARD), 0) <= lax.broadcasted_iota(jnp.int32, (SHARD, SHARD), 1), 1.0, 0.0
    ).astype(bf16)
    named8 = jnp.broadcast_to(named, (16, SHARD))
    rank = jnp.dot(named8.astype(bf16), before, preferred_element_type=f32) * named8
    rank_column = rank.T[:, 0:1]
    capacity = routed.shape[0]
    select = jnp.where(
        lax.broadcasted_iota(jnp.int32, (capacity, SHARD), 0).astype(f32) + 1.0 == rank[0:1, :], 1.0, 0.0
    ).astype(bf16)
    spread = jnp.where(
        lax.broadcasted_iota(jnp.int32, (SHARD, capacity), 1).astype(f32) + 1.0 == rank_column, 1.0, 0.0
    ).astype(bf16)
    everyone = normed[...].reshape(SHARD, WIDTH)
    routed[...] = jnp.dot(select, everyone, preferred_element_type=f32).astype(bf16)
    scores = lax.dot_general(everyone, router[...], (((1,), (1,)), ((), ())), preferred_element_type=f32)
    scores = named_by.T / (1.0 + jnp.exp(-scores))
    own = jnp.where(lax.broadcasted_iota(jnp.int32, (SHARD, 16), 1) == place, scores, 0.0)
    share = jnp.sum(own, axis=1, keepdims=True) / jnp.sum(scores, axis=1, keepdims=True)

    def experts(first, count):
        @pl.loop(0, count)
        def _(number):
            both = lax.dot_general(
                routed[...], weights[first + number, 0 : 2 * w_units], (((1,), (1,)), ((), ())),
                preferred_element_type=f32,
            )
            gated = both[:, 0:w_units]
            upward = both[:, w_units:]
            units_of[number, :, 0:w_units] = (gated / (1.0 + jnp.exp(-gated)) * upward).astype(bf16)

        down_rows = 3 * w_units + 8 - 2 * w_units

        @pl.loop(0, 4)
        def _(number):
            columns = pl.ds(pl.multiple_of(number * 512, 512), 512)
            blank = jnp.zeros((128 - down_rows, 512), bf16)
            left = jnp.concatenate([units_of[chunk] for chunk in range(count)], axis=1)
            right = jnp.concatenate(
                [
                    rows_of
                    for chunk in range(count)
                    for rows_of in (weights[first + chunk, 2 * w_units :, columns], blank)
                ],
                axis=0,
            )
            term = jnp.dot(left, right, preferred_element_type=f32)
            if first == 0:
                result[:, columns] = term
            else:
                result[:, columns] += term

    w_gather.arrive(4)
    experts(0, 5)
    w_gather.arrive(7, 10, 5)
    experts(5, 6)
    w_gather.arrive(13, 8, 11)
    experts(11, 4)
    w_gather.arrive(14)
    experts(15, 1)

    for column in range(4):
        columns = slice(column * 512, column * 512 + 512)
        term = jnp.dot(spread, result[:, columns].astype(bf16), preferred_element_type=f32) * share
        part[:, :, columns] = term.astype(bf16).reshape(16, SLOTS, 512)
    ring_scatter(part, sib2, out_buf2, in_buf2, total, b_send, b_recv, bs_send, bs_recv)
    live = lax.broadcasted_iota(jnp.int32, (SLOTS, 128), 0).astype(f32) < jnp.max(
        jnp.where(row16 == place, tally, 0.0), axis=0, keepdims=True
    )
    change = jnp.where(jnp.where(live, 1.0, 0.0)[:, 0:1] > 0, total[...] + head[...], 0.0)
    delta[...] = change
    logit = jnp.sum(picked[...].astype(f32) * depth_router[...].astype(f32), axis=1, keepdims=True)
    update = change / (1.0 + jnp.exp(-logit))
    high = update.astype(bf16)
    low = (update - high.astype(f32)).astype(bf16)
    back = jnp.where(lax.broadcasted_iota(jnp.int32, (tokens.shape[0], SLOTS), 0) == mine, 1.0, 0.0).astype(bf16)
    added = jnp.dot(back, high, preferred_element_type=f32) + jnp.dot(back, low, preferred_element_type=f32)
    mixed[...] = (tokens[...].astype(f32) + added).astype(bf16)

    for shift in (1, 2, 3):
        count_copy(shift).wait_send()
    for direction, half, hop in ((1, 0, 0), (1, 0, 1), (1, 1, 0), (-1, 1, 0), (-1, 1, 1), (-1, 0, 0)):
        for copy in term_copies(direction, half, hop)[0]:
            copy.wait_send()
    kv_gather.finish()
    q_gather.finish()
    w_gather.finish()


def dma(count):
    return pltpu.SemaphoreType.DMA((count,))


GATHER_SEMS = [dma(16), dma(16), dma(17), dma(17)]
SCATTER_BUFS = [
    pltpu.VMEM((RING, SLOTS, WIDTH), jnp.bfloat16),
    pltpu.VMEM((16, SLOTS, HALF), jnp.bfloat16),
    pltpu.VMEM((16, SLOTS, HALF), jnp.bfloat16),
]
SCATTER_SEMS = [dma(16), dma(16), dma(8), dma(8)]
SMEM = pl.BlockSpec(memory_space=pltpu.SMEM)
ANY = pl.BlockSpec(memory_space=pl.ANY)
CAPACITY = 416


def local(
    tokens, pick_rows, pick_counts, expert_ids, norm_gains, depth_router,
    w_query, w_keyval, w_out, expert_router, w_expert,
):
    f32, bf16 = jnp.float32, jnp.bfloat16
    units = w_expert.shape[3]
    return pl.pallas_call(
        block_kernel,
        out_shape=(
            jax.ShapeDtypeStruct(tokens.shape, bf16),
            jax.ShapeDtypeStruct((SLOTS, WIDTH), f32),
        ),
        in_specs=[VMEM, VMEM, SMEM] + [VMEM] * 3 + [ANY] * 3 + [VMEM] * 2,
        out_specs=(VMEM,) * 2,
        scratch_shapes=[
            pltpu.VMEM((WIDTH, HEAD_DIM), bf16),
            pltpu.VMEM((2, WIDTH, HEAD_DIM), bf16),
            pltpu.VMEM((HEAD_DIM, WIDTH), bf16),
            pltpu.VMEM((SLOTS, WIDTH), bf16),
            pltpu.VMEM((SLOTS, WIDTH), f32),
            pltpu.VMEM((16, SLOTS, WIDTH), bf16),
            pltpu.VMEM((SIDE, 2, SHARD // 2, 2 * HEAD_DIM), bf16),
            pltpu.VMEM((SIDE, 2, SHARD // 2, HEAD_DIM), bf16),
            pltpu.VMEM((SIDE, 16, 128), f32),
            pltpu.VMEM((SIDE, 2, SHARD // 2, 2 * HEAD_DIM), f32),
            pltpu.VMEM((6, SHARD // 2, HEAD_DIM), bf16),
            pltpu.VMEM((6, SHARD // 2, HEAD_DIM), bf16),
            pltpu.VMEM((6, 8, SHARD // 2), f32),
            pltpu.VMEM((6, 8, SHARD // 2), f32),
            pltpu.VMEM((SHARD, HEAD_DIM), bf16),
            pltpu.VMEM((16, 3 * units + 8, WIDTH), bf16),
            pltpu.VMEM((16, SLOTS, WIDTH), bf16),
        ]
        + SCATTER_BUFS
        + [
            pltpu.VMEM((SLOTS, WIDTH), f32),
            pltpu.VMEM((16, SLOTS, WIDTH), bf16),
            pltpu.VMEM((CAPACITY, WIDTH), bf16),
            pltpu.VMEM((6, CAPACITY, 128), bf16),
            pltpu.VMEM((CAPACITY, WIDTH), f32),
        ]
        + SCATTER_BUFS
        + [dma(3)]
        + GATHER_SEMS
        + [dma(6) for _ in range(8)]
        + [dma(3), dma(3), dma(60), dma(60)]
        + SCATTER_SEMS
        + GATHER_SEMS
        + SCATTER_SEMS,
        compiler_params=pltpu.CompilerParams(collective_id=0, has_side_effects=True, vmem_limit_bytes=60 << 20),
        name="block",
    )(
        tokens, pick_rows, pick_counts, expert_ids.T, norm_gains, depth_router[None, :], w_query, w_keyval, w_out,
        expert_router.T, jnp.transpose(w_expert[0], (0, 2, 1)),
    )


def solution(mesh):
    in_specs = (
        P(("seq", "exp"), None), P("seq", None), P("seq"), P("seq", None), P(), P(),
        P(None, "exp"), P(None, None, "exp"), P("exp", None), P(), P("exp", None, None, "seq"),
    )
    out_specs = (P(("seq", "exp"), None), P(("seq", "exp"), None))
    return jax.shard_map(local, mesh=mesh, in_specs=in_specs, out_specs=out_specs, check_vma=False)
```

```python
import functools
import math

import jax
import jax.numpy as jnp
from jax import lax
from jax.experimental import pallas as pl
from jax.experimental.pallas import tpu as pltpu
from jax.sharding import PartitionSpec as P

HEAD_DIM = 128
softcap_limit = 20.0
MESH = pl.DeviceIdType.MESH
SIDE = 4
RING = 8
SLOTS = 48
SHARD = 768
WIDTH = 2048
HALF = 1024
QUARTER = 192
VMEM = pl.BlockSpec(memory_space=pltpu.VMEM)


def wrap(value, size):
    return lax.rem(value + size, size)


def hops(direction, half):
    return 4 if (direction > 0) == (half == 0) else 3


def hop_number(direction, half, hop):
    return ((0 if direction > 0 else 1) * 2 + half) * 4 + hop - 1


def at_exp(index):
    return {"exp": index}


def ring_place():
    place = lax.axis_index("exp")
    return lax.div(place, 2), lax.rem(place, 2)


def greet(partners):
    barrier = pltpu.get_barrier_semaphore()
    for partner in partners:
        pl.semaphore_signal(barrier, inc=1, device_id=partner, device_id_type=MESH)
    pl.semaphore_wait(barrier, len(partners))


def ring_partners():
    z, core = ring_place()
    return [
        at_exp(2 * wrap(z + 1, RING) + core),
        at_exp(2 * wrap(z - 1, RING) + core),
        at_exp(2 * z + 1 - core),
    ]


def remote(src, dst, send, recv, target):
    return pltpu.make_async_remote_copy(
        src_ref=src, dst_ref=dst, send_sem=send, recv_sem=recv, device_id=target, device_id_type=MESH
    )


def ring_gather(buf, send, recv, sib_send, sib_recv, between=lambda hop: None):
    z, core = ring_place()
    sibling = at_exp(2 * z + 1 - core)

    def part(origin, side, half):
        return buf.at[2 * origin + side, :, pl.ds(half * HALF, HALF)]

    def hop_copy(direction, half, hop, arriving):
        origin = wrap(z - direction * (hop if arriving else hop - 1), RING)
        ref = part(origin, core, half)
        number = hop_number(direction, half, hop)
        return remote(ref, ref, send.at[number], recv.at[number], at_exp(2 * wrap(z + direction, RING) + core))

    def sib_copy(direction, half, hop, arriving):
        origin = wrap(z - direction * hop, RING)
        ref = part(origin, 1 - core if arriving else core, half)
        number = hop_number(direction, half, hop)
        return remote(ref, ref, sib_send.at[number], sib_recv.at[number], sibling)

    def own_copy(arriving):
        ref = buf.at[2 * z + (1 - core if arriving else core)]
        return remote(ref, ref, sib_send.at[16], sib_recv.at[16], sibling)

    lanes = [(1, 0), (-1, 1), (1, 1), (-1, 0)]
    for direction, half in lanes:
        hop_copy(direction, half, 1, False).start()
    own_copy(False).start()
    for hop in range(1, 5):
        for direction, half in lanes:
            if hop <= hops(direction, half):
                hop_copy(direction, half, hop, True).wait_recv()
                if hop < hops(direction, half):
                    hop_copy(direction, half, hop + 1, False).start()
                sib_copy(direction, half, hop, False).start()
        between(hop)
    own_copy(True).wait_recv()
    own_copy(False).wait_send()
    for hop in range(1, 5):
        for direction, half in lanes:
            if hop <= hops(direction, half):
                sib_copy(direction, half, hop, True).wait_recv()
                sib_copy(direction, half, hop, False).wait_send()
                hop_copy(direction, half, hop, False).wait_send()


def ring_scatter(part, sib, out_buf, in_buf, total, send, recv, sib_send, sib_recv, between=lambda hop: None):
    z, core = ring_place()
    sibling = at_exp(2 * z + 1 - core)

    def sib_copy(offset):
        target = wrap(z + offset, RING)
        return remote(
            part.at[2 * target + 1 - core], sib.at[target], sib_send.at[offset % RING], sib_recv.at[offset % RING], sibling
        )

    def mine(target, half):
        columns = pl.ds(half * HALF, HALF)
        return part[2 * target + core, :, columns].astype(jnp.float32) + sib[target, :, columns].astype(jnp.float32)

    def hop_copy(direction, half, hop):
        number = hop_number(direction, half, hop)
        return remote(
            out_buf.at[number], in_buf.at[number], send.at[number], recv.at[number],
            at_exp(2 * wrap(z + direction, RING) + core),
        )

    order = [4, 3, -3, 2, -2, 1, -1, 0]
    for offset in order:
        sib_copy(offset).start()
    arrived = set()
    lanes = [(1, 0), (-1, 1), (1, 1), (-1, 0)]

    def have(offset):
        if offset % RING not in arrived:
            arrived.add(offset % RING)
            sib_copy(offset).wait_recv()

    for hop in range(1, 5):
        for direction, half in lanes:
            last = hops(direction, half)
            if hop <= last:
                offset = direction * (last - hop + 1)
                have(offset)
                number = hop_number(direction, half, hop)
                value = mine(wrap(z + offset, RING), half)
                if hop > 1:
                    hop_copy(direction, half, hop - 1).wait_recv()
                    value = value + in_buf[number - 1].astype(jnp.float32)
                out_buf[number] = value.astype(jnp.bfloat16)
                hop_copy(direction, half, hop).start()
        between(hop)
    have(0)
    for half in range(2):
        value = mine(z, half)
        for direction in (1, -1):
            last = hops(direction, half)
            hop_copy(direction, half, last).wait_recv()
            value = value + in_buf[hop_number(direction, half, last)].astype(jnp.float32)
        total[:, half * HALF : (half + 1) * HALF] = value
    for offset in order:
        sib_copy(offset).wait_send()
    for direction, half in lanes:
        for hop in range(1, hops(direction, half) + 1):
            hop_copy(direction, half, hop).wait_send()


def normalize(widened, gain):
    scale = lax.rsqrt(jnp.mean(widened * widened, axis=-1, keepdims=True) + 1e-06)
    return (widened * scale * gain).astype(jnp.bfloat16)


def live_lanes(counts):
    row = lax.broadcasted_iota(jnp.int32, (SHARD, 16), 0)
    first = lax.broadcasted_iota(jnp.int32, (SHARD, 16), 1) * SLOTS
    spread = jnp.where((row >= first) & (row < first + SLOTS), 1.0, 0.0).astype(jnp.bfloat16)
    block = lax.broadcasted_iota(jnp.int32, (16, 128), 0).astype(jnp.float32)
    count_of = jnp.dot(spread, counts.astype(jnp.bfloat16), preferred_element_type=jnp.float32)
    block_of = jnp.dot(spread, block.astype(jnp.bfloat16), preferred_element_type=jnp.float32)
    slot = lax.broadcasted_iota(jnp.int32, (SHARD, 128), 0).astype(jnp.float32) - block_of * SLOTS
    return jnp.where(slot < count_of, 1.0, 0.0)


ORDER = [
    (0, 0), (1, 0), (-1, 0), (0, 1), (0, -1), (1, 1), (1, -1), (-1, 1), (-1, -1), (2, 0), (0, 2),
    (2, 1), (2, -1), (1, 2), (-1, 2), (2, 2),
]


def offset_slot(dx, dy):
    return ORDER.index((((dx + 1) % SIDE) - 1, ((dy + 1) % SIDE) - 1))


def torus_place():
    place = lax.axis_index("seq")
    return lax.div(place, SIDE), lax.rem(place, SIDE)


def at_torus(px, py):
    return {"seq": wrap(px, SIDE) * SIDE + wrap(py, SIDE)}


def along(axis, step):
    x, y = torus_place()
    return at_torus(x + step, y) if axis == 0 else at_torus(x, y + step)


class TorusGather:
    def __init__(self, block, send, recv):
        self.block, self.send, self.recv = block, send, recv
        self.x, self.y = torus_place()

    def copy(self, quarter, number):
        d = 1 if quarter % 2 == 0 else -1
        line, kind = (0, number) if number < 3 else divmod(number - 3, 3)
        step = -d if kind == 1 else d
        along = [-d, d, -2 * d][kind]
        if number < 3:
            origin, move = (along, 0), (step, 0)
        else:
            origin, move = ([0, -d, d, -2 * d][line], along), (0, step)
        source = (origin[0] + move[0], origin[1] + move[1])
        if quarter < 2:
            origin, move, source = origin[::-1], move[::-1], source[::-1]
        place = quarter * 15 + number
        return remote(
            self.block(offset_slot(*source), quarter), self.block(offset_slot(*origin), quarter),
            self.send.at[place], self.recv.at[place], at_torus(self.x + move[0], self.y + move[1]),
        )

    def start(self, quarter, *numbers):
        for number in numbers:
            self.copy(quarter, number).start()

    def arrive(self, *numbers):
        for number in numbers:
            for quarter in range(4):
                self.copy(quarter, number).wait_recv()

    def stage(self, stage, quarters=range(4)):
        for quarter in quarters:
            for needed, following in [
                [(None, (0, 1, 3, 4))],
                [(0, (2, 6, 7)), (1, (9, 10)), (3, (5,))],
                [(2, (12, 13)), (6, (8,)), (9, (11,))],
                [(12, (14,))],
            ][stage]:
                if needed is not None:
                    self.copy(quarter, needed).wait_recv()
                self.start(quarter, *following)

    def finish(self):
        for quarter in range(4):
            for number in range(15):
                self.copy(quarter, number).wait_send()


class LineGather:
    def __init__(self, axis, block, send, recv):
        self.axis, self.block, self.send, self.recv = axis, block, send, recv

    def copy(self, half, number):
        d = 1 if half == 0 else -1
        step = -d if number == 1 else d
        origin = [-d, d, -2 * d][number]
        place = half * 3 + number
        return remote(
            self.block((origin + step) % SIDE, half), self.block(origin % SIDE, half),
            self.send.at[place], self.recv.at[place], along(self.axis, step),
        )

    def begin(self):
        for half in range(2):
            self.copy(half, 0).start()
            self.copy(half, 1).start()

    def forward(self):
        for half in range(2):
            self.copy(half, 0).wait_recv()
            self.copy(half, 2).start()
        for half in range(2):
            self.copy(half, 1).wait_recv()

    def last(self):
        for half in range(2):
            self.copy(half, 2).wait_recv()

    def finish(self):
        for half in range(2):
            for number in range(3):
                self.copy(half, number).wait_send()


def block_kernel(
    tokens, rows, counts, ids, gains, depth_router, w_query_hbm, w_keyval_hbm, w_out_hbm, router, w_expert,
    mixed, delta,
    w_query, w_keyval, w_out, picked, total, gathered, kv, query, tallies, acc, term_out, term_in, mass_out, mass_in,
    attended, weights, part, sib, out_buf, in_buf, head, normed, routed, units_of, result,
    sib2, out_buf2, in_buf2,
    local_sem, g_send, g_recv, gs_send, gs_recv, kv_send, kv_recv, q_send, q_recv, t_send, t_recv, m_send, m_recv,
    count_send, count_recv, w_send, w_recv,
    r_send, r_recv, rs_send, rs_recv, n_send, n_recv, ns_send, ns_recv, b_send, b_recv, bs_send, bs_recv,
):
    f32, bf16 = jnp.float32, jnp.bfloat16
    place = lax.axis_index("exp")
    seq = lax.axis_index("seq")
    w_units = w_expert.shape[1]
    x, y = torus_place()
    loads = [
        pltpu.make_async_copy(source, target, local_sem.at[number])
        for number, (source, target) in enumerate(
            ((w_keyval_hbm, w_keyval), (w_query_hbm, w_query), (w_out_hbm, w_out))
        )
    ]
    for load in loads:
        load.start()
    weights[0, 0 : w_units] = w_expert[0]
    weights[0, w_units : 2 * w_units] = w_expert[1]
    weights[0, 2 * w_units :] = jnp.zeros_like(weights[0, 2 * w_units :])
    weights[0, 2 * w_units : 3 * w_units] = w_expert[2]
    greet(
        ring_partners()
        + [at_torus(x + dx, y + dy) for dx, dy in ((0, 1), (0, -1), (0, 2), (1, 0), (-1, 0))]
    )

    w_gather = TorusGather(lambda slot, quarter: weights.at[slot, :, pl.ds(quarter * 512, 512)], w_send, w_recv)

    w_gather.stage(0, range(4))
    row16 = lax.broadcasted_iota(jnp.int32, (16, 128), 0)
    tally = jnp.zeros((16, 128), f32)
    for device in range(16):
        tally = jnp.where(row16 == device, counts[device].astype(f32), tally)
    tallies[0] = tally

    def count_copy(shift):
        return remote(
            tallies.at[0], tallies.at[SIDE - shift], count_send.at[shift - 1], count_recv.at[shift - 1],
            at_torus(x, y + shift),
        )

    for shift in (1, 2, 3):
        count_copy(shift).start()
    acc[...] = jnp.zeros_like(acc)
    units_of[...] = jnp.zeros_like(units_of)

    mine = rows[pl.ds(place, 1), :]
    onehot = jnp.where(
        lax.broadcasted_iota(jnp.int32, (tokens.shape[0], SLOTS), 0) == mine, 1.0, 0.0
    ).T.astype(bf16)
    chosen = jnp.dot(onehot, tokens[...], preferred_element_type=f32)
    picked[...] = chosen.astype(bf16)
    gathered[place] = normalize(chosen, gains[0:1, :])
    ring_gather(gathered, g_send, g_recv, gs_send, gs_recv)
    for load in loads:
        load.wait()
    half_rows = SHARD // 2
    inputs = gathered[...].reshape(SHARD, WIDTH)
    keys = jnp.dot(inputs, w_keyval[0], preferred_element_type=f32).astype(bf16)
    values = jnp.dot(inputs, w_keyval[1], preferred_element_type=f32)
    values = (values * live_lanes(tally)).astype(bf16)
    kv[0, :, :, 0:HEAD_DIM] = keys.reshape(2, half_rows, HEAD_DIM)
    kv[0, :, :, HEAD_DIM:] = values.reshape(2, half_rows, HEAD_DIM)
    kv_gather = LineGather(1, lambda offset, half: kv.at[offset, half], kv_send, kv_recv)
    kv_gather.begin()
    queries = jnp.dot(inputs, w_query[...], preferred_element_type=f32).astype(bf16)
    query[0] = queries.reshape(2, half_rows, HEAD_DIM)
    q_gather = LineGather(0, lambda offset, half: query.at[offset, half], q_send, q_recv)
    q_gather.begin()

    c1 = HEAD_DIM ** (-0.5) / softcap_limit
    c2 = softcap_limit * math.log2(math.e)
    tile = 384

    def unit(dx, dy, diagonal=False):
        unit_keys = kv[dy, :, :, 0:HEAD_DIM].reshape(SHARD, HEAD_DIM)
        live = live_lanes(tallies[dy]).astype(bf16)
        unit_values = jnp.concatenate([kv[dy, :, :, HEAD_DIM:].reshape(SHARD, HEAD_DIM), live], axis=1)

        for half in range(2):

            @pl.loop(0, half_rows // tile)
            def _(number):
                first = pl.multiple_of(number * tile, tile)
                scores = lax.dot_general(
                    query[dx, half, pl.ds(first, tile), :], unit_keys, (((1,), (1,)), ((), ())),
                    preferred_element_type=f32,
                )
                weight = jnp.exp2(c2 * jnp.tanh(scores * c1))
                if diagonal:
                    row = lax.broadcasted_iota(jnp.int32, (tile, SHARD), 0) + first + half * half_rows
                    column = lax.broadcasted_iota(jnp.int32, (tile, SHARD), 1)
                    weight = jnp.where(column <= row, weight, 0.0)
                acc[dx, half, pl.ds(first, tile), :] += jnp.dot(
                    weight.astype(bf16), unit_values, preferred_element_type=f32
                )

    def earlier(dx, dy):
        @pl.when((wrap(x + dx, SIDE) > x) if dx else (wrap(y + dy, SIDE) < y))
        def _():
            unit(dx, dy)

    unit(0, 0, True)

    named_by = jnp.concatenate(
        [
            jnp.max(jnp.where(ids[...] == expert, 1.0, 0.0), axis=0, keepdims=True)
            for expert in range(16)
        ],
        axis=0,
    )
    named = jnp.max(jnp.where(ids[...] == place, 1.0, 0.0), axis=0, keepdims=True)
    before = jnp.where(
        lax.broadcasted_iota(jnp.int32, (SHARD, SHARD), 0) <= lax.broadcasted_iota(jnp.int32, (SHARD, SHARD), 1), 1.0, 0.0
    ).astype(bf16)
    named8 = jnp.broadcast_to(named, (16, SHARD))
    rank = jnp.dot(named8.astype(bf16), before, preferred_element_type=f32) * named8
    rank_column = rank.T[:, 0:1]
    capacity = routed.shape[0]
    select = jnp.where(
        lax.broadcasted_iota(jnp.int32, (capacity, SHARD), 0).astype(f32) + 1.0 == rank[0:1, :], 1.0, 0.0
    ).astype(bf16)
    spread = jnp.where(
        lax.broadcasted_iota(jnp.int32, (SHARD, capacity), 1).astype(f32) + 1.0 == rank_column, 1.0, 0.0
    ).astype(bf16)

    q_gather.forward()
    kv_gather.forward()
    earlier(1, 0)
    earlier(3, 0)
    for shift in (1, 2, 3):
        count_copy(shift).wait_recv()
    q_gather.last()
    earlier(2, 0)
    for dy in (1, 3):
        for dx in (2, 1, 3, 0):
            earlier(dx, dy)
    kv_gather.last()
    earlier(2, 2)

    def term_copies(direction, half, hop):
        number = (0 if direction > 0 else 3) + (hop if half == (0 if direction > 0 else 1) else 2)
        target = along(0, direction)
        return (
            remote(term_out.at[number], term_in.at[number], t_send.at[number], t_recv.at[number], target),
            remote(mass_out.at[number], mass_in.at[number], m_send.at[number], m_recv.at[number], target),
        ), number

    def send_terms(direction, half, hop, dx, received):
        copies, number = term_copies(direction, half, hop)
        value = acc[dx, half, :, 0:HEAD_DIM]
        mass = acc[dx, half, :, HEAD_DIM:].T[0:8, :]
        if received is not None:
            value = value + term_in[received].astype(f32)
            mass = mass + mass_in[received]
        term_out[number] = value.astype(bf16)
        mass_out[number] = mass
        for copy in copies:
            copy.start()

    def take_terms(direction, half, hop):
        copies, number = term_copies(direction, half, hop)
        for copy in copies:
            copy.wait_recv()
        return number

    send_terms(1, 0, 0, 2, None)
    send_terms(-1, 1, 0, 2, None)
    earlier(1, 2)
    earlier(3, 2)
    send_terms(1, 1, 0, 1, None)
    send_terms(-1, 0, 0, 3, None)
    send_terms(1, 0, 1, 1, take_terms(1, 0, 0))
    send_terms(-1, 1, 1, 3, take_terms(-1, 1, 0))
    w_gather.stage(1, range(4))
    earlier(0, 2)
    for half in range(2):
        value = acc[0, half, :, 0:HEAD_DIM]
        mass = acc[0, half, :, HEAD_DIM:]
        for direction in (-1, 1):
            number = take_terms(direction, half, 1 if half == (0 if direction > 0 else 1) else 0)
            value = value + term_in[number].astype(f32)
            mass = mass + jnp.broadcast_to(mass_in[number].T[:, 0:1], mass.shape)
        attended[half * half_rows : (half + 1) * half_rows, :] = (
            value / jnp.where(mass > 0, mass, 1.0)
        ).astype(bf16)

    @pl.loop(0, 4)
    def _(number):
        block = attended[pl.ds(pl.multiple_of(number * 4 * SLOTS, 4 * SLOTS), 4 * SLOTS), :]
        sums = jnp.dot(block, w_out[...], preferred_element_type=f32).astype(bf16)
        part[pl.ds(number * 4, 4)] = sums.reshape(4, SLOTS, WIDTH)

    def during_scatter(hop):
        pass

    def during_gather(hop):
        if hop == 1:
            w_gather.stage(2, (0,))
        if hop == 2:
            w_gather.stage(2, (2,))
        if hop == 3:
            w_gather.stage(2, (1,3))

    ring_scatter(part, sib, out_buf, in_buf, head, r_send, r_recv, rs_send, rs_recv, during_scatter)
    normed[place] = normalize(picked[...].astype(f32) + head[...], gains[1:2, :])
    ring_gather(normed, n_send, n_recv, ns_send, ns_recv, during_gather)

    everyone = normed[...].reshape(SHARD, WIDTH)
    routed[...] = jnp.dot(select, everyone, preferred_element_type=f32).astype(bf16)
    scores = lax.dot_general(everyone, router[...], (((1,), (1,)), ((), ())), preferred_element_type=f32)
    scores = named_by.T / (1.0 + jnp.exp(-scores))
    own = jnp.where(lax.broadcasted_iota(jnp.int32, (SHARD, 16), 1) == place, scores, 0.0)
    share = jnp.sum(own, axis=1, keepdims=True) / jnp.sum(scores, axis=1, keepdims=True)

    def experts(first, count):
        @pl.loop(0, count)
        def _(number):
            both = lax.dot_general(
                routed[...], weights[first + number, 0 : 2 * w_units], (((1,), (1,)), ((), ())),
                preferred_element_type=f32,
            )
            gated = both[:, 0:w_units]
            upward = both[:, w_units:]
            units_of[number, :, 0:w_units] = (gated / (1.0 + jnp.exp(-gated)) * upward).astype(bf16)

        down_rows = 3 * w_units + 8 - 2 * w_units

        @pl.loop(0, 4)
        def _(number):
            columns = pl.ds(pl.multiple_of(number * 512, 512), 512)
            blank = jnp.zeros((128 - down_rows, 512), bf16)
            left = jnp.concatenate([units_of[chunk] for chunk in range(count)], axis=1)
            right = jnp.concatenate(
                [
                    rows_of
                    for chunk in range(count)
                    for rows_of in (weights[first + chunk, 2 * w_units :, columns], blank)
                ],
                axis=0,
            )
            term = jnp.dot(left, right, preferred_element_type=f32)
            if first == 0:
                result[:, columns] = term
            else:
                result[:, columns] += term

    w_gather.arrive(4)
    experts(0, 5)
    w_gather.stage(3, range(4))
    w_gather.arrive(7, 10, 5)
    experts(5, 6)
    w_gather.arrive(13, 8, 11)
    experts(11, 4)
    w_gather.arrive(14)
    experts(15, 1)

    for column in range(4):
        columns = slice(column * 512, column * 512 + 512)
        term = jnp.dot(spread, result[:, columns].astype(bf16), preferred_element_type=f32) * share
        part[:, :, columns] = term.astype(bf16).reshape(16, SLOTS, 512)
    ring_scatter(part, sib2, out_buf2, in_buf2, total, b_send, b_recv, bs_send, bs_recv)
    live = lax.broadcasted_iota(jnp.int32, (SLOTS, 128), 0).astype(f32) < jnp.max(
        jnp.where(row16 == place, tally, 0.0), axis=0, keepdims=True
    )
    change = jnp.where(jnp.where(live, 1.0, 0.0)[:, 0:1] > 0, total[...] + head[...], 0.0)
    delta[...] = change
    logit = jnp.sum(picked[...].astype(f32) * depth_router[...].astype(f32), axis=1, keepdims=True)
    update = change / (1.0 + jnp.exp(-logit))
    high = update.astype(bf16)
    low = (update - high.astype(f32)).astype(bf16)
    back = jnp.where(lax.broadcasted_iota(jnp.int32, (tokens.shape[0], SLOTS), 0) == mine, 1.0, 0.0).astype(bf16)
    added = jnp.dot(back, high, preferred_element_type=f32) + jnp.dot(back, low, preferred_element_type=f32)
    mixed[...] = (tokens[...].astype(f32) + added).astype(bf16)

    for shift in (1, 2, 3):
        count_copy(shift).wait_send()
    for direction, half, hop in ((1, 0, 0), (1, 0, 1), (1, 1, 0), (-1, 1, 0), (-1, 1, 1), (-1, 0, 0)):
        for copy in term_copies(direction, half, hop)[0]:
            copy.wait_send()
    kv_gather.finish()
    q_gather.finish()
    w_gather.finish()


def dma(count):
    return pltpu.SemaphoreType.DMA((count,))


GATHER_SEMS = [dma(16), dma(16), dma(17), dma(17)]
SCATTER_BUFS = [
    pltpu.VMEM((RING, SLOTS, WIDTH), jnp.bfloat16),
    pltpu.VMEM((16, SLOTS, HALF), jnp.bfloat16),
    pltpu.VMEM((16, SLOTS, HALF), jnp.bfloat16),
]
SCATTER_SEMS = [dma(16), dma(16), dma(8), dma(8)]
SMEM = pl.BlockSpec(memory_space=pltpu.SMEM)
ANY = pl.BlockSpec(memory_space=pl.ANY)
CAPACITY = 416


def local(
    tokens, pick_rows, pick_counts, expert_ids, norm_gains, depth_router,
    w_query, w_keyval, w_out, expert_router, w_expert,
):
    f32, bf16 = jnp.float32, jnp.bfloat16
    units = w_expert.shape[3]
    return pl.pallas_call(
        block_kernel,
        out_shape=(
            jax.ShapeDtypeStruct(tokens.shape, bf16),
            jax.ShapeDtypeStruct((SLOTS, WIDTH), f32),
        ),
        in_specs=[VMEM, VMEM, SMEM] + [VMEM] * 3 + [ANY] * 3 + [VMEM] * 2,
        out_specs=(VMEM,) * 2,
        scratch_shapes=[
            pltpu.VMEM((WIDTH, HEAD_DIM), bf16),
            pltpu.VMEM((2, WIDTH, HEAD_DIM), bf16),
            pltpu.VMEM((HEAD_DIM, WIDTH), bf16),
            pltpu.VMEM((SLOTS, WIDTH), bf16),
            pltpu.VMEM((SLOTS, WIDTH), f32),
            pltpu.VMEM((16, SLOTS, WIDTH), bf16),
            pltpu.VMEM((SIDE, 2, SHARD // 2, 2 * HEAD_DIM), bf16),
            pltpu.VMEM((SIDE, 2, SHARD // 2, HEAD_DIM), bf16),
            pltpu.VMEM((SIDE, 16, 128), f32),
            pltpu.VMEM((SIDE, 2, SHARD // 2, 2 * HEAD_DIM), f32),
            pltpu.VMEM((6, SHARD // 2, HEAD_DIM), bf16),
            pltpu.VMEM((6, SHARD // 2, HEAD_DIM), bf16),
            pltpu.VMEM((6, 8, SHARD // 2), f32),
            pltpu.VMEM((6, 8, SHARD // 2), f32),
            pltpu.VMEM((SHARD, HEAD_DIM), bf16),
            pltpu.VMEM((16, 3 * units + 8, WIDTH), bf16),
            pltpu.VMEM((16, SLOTS, WIDTH), bf16),
        ]
        + SCATTER_BUFS
        + [
            pltpu.VMEM((SLOTS, WIDTH), f32),
            pltpu.VMEM((16, SLOTS, WIDTH), bf16),
            pltpu.VMEM((CAPACITY, WIDTH), bf16),
            pltpu.VMEM((6, CAPACITY, 128), bf16),
            pltpu.VMEM((CAPACITY, WIDTH), f32),
        ]
        + SCATTER_BUFS
        + [dma(3)]
        + GATHER_SEMS
        + [dma(6) for _ in range(8)]
        + [dma(3), dma(3), dma(60), dma(60)]
        + SCATTER_SEMS
        + GATHER_SEMS
        + SCATTER_SEMS,
        compiler_params=pltpu.CompilerParams(collective_id=0, has_side_effects=True, vmem_limit_bytes=60 << 20),
        name="block",
    )(
        tokens, pick_rows, pick_counts, expert_ids.T, norm_gains, depth_router[None, :], w_query, w_keyval, w_out,
        expert_router.T, jnp.transpose(w_expert[0], (0, 2, 1)),
    )


def solution(mesh):
    in_specs = (
        P(("seq", "exp"), None), P("seq", None), P("seq"), P("seq", None), P(), P(),
        P(None, "exp"), P(None, None, "exp"), P("exp", None), P(), P("exp", None, None, "seq"),
    )
    out_specs = (P(("seq", "exp"), None), P(("seq", "exp"), None))
    return jax.shard_map(local, mesh=mesh, in_specs=in_specs, out_specs=out_specs, check_vma=False)
```

```python
import functools
import math

import jax
import jax.numpy as jnp
from jax import lax
from jax.experimental import pallas as pl
from jax.experimental.pallas import tpu as pltpu
from jax.sharding import PartitionSpec as P

HEAD_DIM = 128
softcap_limit = 20.0
MESH = pl.DeviceIdType.MESH
SIDE = 4
RING = 8
SLOTS = 48
SHARD = 768
WIDTH = 2048
HALF = 1024
QUARTER = 192
VMEM = pl.BlockSpec(memory_space=pltpu.VMEM)


def wrap(value, size):
    return lax.rem(value + size, size)


def hops(direction, half):
    return 4 if (direction > 0) == (half == 0) else 3


def hop_number(direction, half, hop):
    return ((0 if direction > 0 else 1) * 2 + half) * 4 + hop - 1


def at_exp(index):
    return {"exp": index}


def ring_place():
    place = lax.axis_index("exp")
    return lax.div(place, 2), lax.rem(place, 2)


def greet(partners):
    barrier = pltpu.get_barrier_semaphore()
    for partner in partners:
        pl.semaphore_signal(barrier, inc=1, device_id=partner, device_id_type=MESH)
    pl.semaphore_wait(barrier, len(partners))


def ring_partners():
    z, core = ring_place()
    return [
        at_exp(2 * wrap(z + 1, RING) + core),
        at_exp(2 * wrap(z - 1, RING) + core),
        at_exp(2 * z + 1 - core),
    ]


def remote(src, dst, send, recv, target):
    return pltpu.make_async_remote_copy(
        src_ref=src, dst_ref=dst, send_sem=send, recv_sem=recv, device_id=target, device_id_type=MESH
    )


def ring_gather(buf, send, recv, sib_send, sib_recv, between=lambda hop: None):
    z, core = ring_place()
    sibling = at_exp(2 * z + 1 - core)

    def part(origin, side, half):
        return buf.at[2 * origin + side, :, pl.ds(half * HALF, HALF)]

    def hop_copy(direction, half, hop, arriving):
        origin = wrap(z - direction * (hop if arriving else hop - 1), RING)
        ref = part(origin, core, half)
        number = hop_number(direction, half, hop)
        return remote(ref, ref, send.at[number], recv.at[number], at_exp(2 * wrap(z + direction, RING) + core))

    def sib_copy(direction, half, hop, arriving):
        origin = wrap(z - direction * hop, RING)
        ref = part(origin, 1 - core if arriving else core, half)
        number = hop_number(direction, half, hop)
        return remote(ref, ref, sib_send.at[number], sib_recv.at[number], sibling)

    def own_copy(arriving):
        ref = buf.at[2 * z + (1 - core if arriving else core)]
        return remote(ref, ref, sib_send.at[16], sib_recv.at[16], sibling)

    lanes = [(1, 0), (-1, 1), (1, 1), (-1, 0)]
    for direction, half in lanes:
        hop_copy(direction, half, 1, False).start()
    own_copy(False).start()
    for hop in range(1, 5):
        for direction, half in lanes:
            if hop <= hops(direction, half):
                hop_copy(direction, half, hop, True).wait_recv()
                if hop < hops(direction, half):
                    hop_copy(direction, half, hop + 1, False).start()
                sib_copy(direction, half, hop, False).start()
        between(hop)
    own_copy(True).wait_recv()
    own_copy(False).wait_send()
    for hop in range(1, 5):
        for direction, half in lanes:
            if hop <= hops(direction, half):
                sib_copy(direction, half, hop, True).wait_recv()
                sib_copy(direction, half, hop, False).wait_send()
                hop_copy(direction, half, hop, False).wait_send()


def ring_scatter(part, sib, out_buf, in_buf, total, send, recv, sib_send, sib_recv, between=lambda hop: None):
    z, core = ring_place()
    sibling = at_exp(2 * z + 1 - core)

    def sib_copy(offset):
        target = wrap(z + offset, RING)
        return remote(
            part.at[2 * target + 1 - core], sib.at[target], sib_send.at[offset % RING], sib_recv.at[offset % RING], sibling
        )

    def mine(target, half):
        columns = pl.ds(half * HALF, HALF)
        return part[2 * target + core, :, columns].astype(jnp.float32) + sib[target, :, columns].astype(jnp.float32)

    def hop_copy(direction, half, hop):
        number = hop_number(direction, half, hop)
        return remote(
            out_buf.at[number], in_buf.at[number], send.at[number], recv.at[number],
            at_exp(2 * wrap(z + direction, RING) + core),
        )

    order = [4, 3, -3, 2, -2, 1, -1, 0]
    for offset in order:
        sib_copy(offset).start()
    arrived = set()
    lanes = [(1, 0), (-1, 1), (1, 1), (-1, 0)]

    def have(offset):
        if offset % RING not in arrived:
            arrived.add(offset % RING)
            sib_copy(offset).wait_recv()

    for hop in range(1, 5):
        for direction, half in lanes:
            last = hops(direction, half)
            if hop <= last:
                offset = direction * (last - hop + 1)
                have(offset)
                number = hop_number(direction, half, hop)
                value = mine(wrap(z + offset, RING), half)
                if hop > 1:
                    hop_copy(direction, half, hop - 1).wait_recv()
                    value = value + in_buf[number - 1].astype(jnp.float32)
                out_buf[number] = value.astype(jnp.bfloat16)
                hop_copy(direction, half, hop).start()
        between(hop)
    have(0)
    for half in range(2):
        value = mine(z, half)
        for direction in (1, -1):
            last = hops(direction, half)
            hop_copy(direction, half, last).wait_recv()
            value = value + in_buf[hop_number(direction, half, last)].astype(jnp.float32)
        total[:, half * HALF : (half + 1) * HALF] = value
    for offset in order:
        sib_copy(offset).wait_send()
    for direction, half in lanes:
        for hop in range(1, hops(direction, half) + 1):
            hop_copy(direction, half, hop).wait_send()


def normalize(widened, gain):
    scale = lax.rsqrt(jnp.mean(widened * widened, axis=-1, keepdims=True) + 1e-06)
    return (widened * scale * gain).astype(jnp.bfloat16)


def live_lanes(counts):
    row = lax.broadcasted_iota(jnp.int32, (SHARD, 16), 0)
    first = lax.broadcasted_iota(jnp.int32, (SHARD, 16), 1) * SLOTS
    spread = jnp.where((row >= first) & (row < first + SLOTS), 1.0, 0.0).astype(jnp.bfloat16)
    block = lax.broadcasted_iota(jnp.int32, (16, 128), 0).astype(jnp.float32)
    count_of = jnp.dot(spread, counts.astype(jnp.bfloat16), preferred_element_type=jnp.float32)
    block_of = jnp.dot(spread, block.astype(jnp.bfloat16), preferred_element_type=jnp.float32)
    slot = lax.broadcasted_iota(jnp.int32, (SHARD, 128), 0).astype(jnp.float32) - block_of * SLOTS
    return jnp.where(slot < count_of, 1.0, 0.0)


ORDER = [
    (0, 0), (1, 0), (-1, 0), (0, 1), (0, -1), (1, 1), (1, -1), (-1, 1), (-1, -1), (2, 0), (0, 2),
    (2, 1), (2, -1), (1, 2), (-1, 2), (2, 2),
]


def offset_slot(dx, dy):
    return ORDER.index((((dx + 1) % SIDE) - 1, ((dy + 1) % SIDE) - 1))


def torus_place():
    place = lax.axis_index("seq")
    return lax.div(place, SIDE), lax.rem(place, SIDE)


def at_torus(px, py):
    return {"seq": wrap(px, SIDE) * SIDE + wrap(py, SIDE)}


def along(axis, step):
    x, y = torus_place()
    return at_torus(x + step, y) if axis == 0 else at_torus(x, y + step)


class TorusGather:
    def __init__(self, block, send, recv):
        self.block, self.send, self.recv = block, send, recv
        self.x, self.y = torus_place()

    def copy(self, quarter, number):
        d = 1 if quarter % 2 == 0 else -1
        line, kind = (0, number) if number < 3 else divmod(number - 3, 3)
        step = -d if kind == 1 else d
        along = [-d, d, -2 * d][kind]
        if number < 3:
            origin, move = (along, 0), (step, 0)
        else:
            origin, move = ([0, -d, d, -2 * d][line], along), (0, step)
        source = (origin[0] + move[0], origin[1] + move[1])
        if quarter < 2:
            origin, move, source = origin[::-1], move[::-1], source[::-1]
        place = quarter * 15 + number
        return remote(
            self.block(offset_slot(*source), quarter), self.block(offset_slot(*origin), quarter),
            self.send.at[place], self.recv.at[place], at_torus(self.x + move[0], self.y + move[1]),
        )

    def start(self, quarter, *numbers):
        for number in numbers:
            self.copy(quarter, number).start()

    def arrive(self, *numbers):
        for number in numbers:
            for quarter in range(4):
                self.copy(quarter, number).wait_recv()

    def stage(self, stage, quarters=range(4)):
        for quarter in quarters:
            for needed, following in [
                [(None, (0, 1, 3, 4))],
                [(0, (2, 6, 7)), (1, (9, 10)), (3, (5,))],
                [(2, (12, 13)), (6, (8,)), (9, (11,))],
                [(12, (14,))],
            ][stage]:
                if needed is not None:
                    self.copy(quarter, needed).wait_recv()
                self.start(quarter, *following)

    def finish(self):
        for quarter in range(4):
            for number in range(15):
                self.copy(quarter, number).wait_send()


class LineGather:
    def __init__(self, axis, block, send, recv):
        self.axis, self.block, self.send, self.recv = axis, block, send, recv

    def copy(self, half, number):
        d = 1 if half == 0 else -1
        step = -d if number == 1 else d
        origin = [-d, d, -2 * d][number]
        place = half * 3 + number
        return remote(
            self.block((origin + step) % SIDE, half), self.block(origin % SIDE, half),
            self.send.at[place], self.recv.at[place], along(self.axis, step),
        )

    def begin(self):
        for half in range(2):
            self.copy(half, 0).start()
            self.copy(half, 1).start()

    def forward(self):
        for half in range(2):
            self.copy(half, 0).wait_recv()
            self.copy(half, 2).start()
        for half in range(2):
            self.copy(half, 1).wait_recv()

    def last(self):
        for half in range(2):
            self.copy(half, 2).wait_recv()

    def finish(self):
        for half in range(2):
            for number in range(3):
                self.copy(half, number).wait_send()


def block_kernel(
    tokens, rows, counts, ids, gains, depth_router, w_query_hbm, w_keyval_hbm, w_out_hbm, router, w_expert,
    mixed, delta,
    w_query, w_keyval, w_out, picked, total, gathered, kv, query, tallies, acc, term_out, term_in, mass_out, mass_in,
    attended, weights, part, sib, out_buf, in_buf, head, normed, routed, units_of, result,
    sib2, out_buf2, in_buf2,
    local_sem, g_send, g_recv, gs_send, gs_recv, kv_send, kv_recv, q_send, q_recv, t_send, t_recv, m_send, m_recv,
    count_send, count_recv, w_send, w_recv,
    r_send, r_recv, rs_send, rs_recv, n_send, n_recv, ns_send, ns_recv, b_send, b_recv, bs_send, bs_recv,
):
    f32, bf16 = jnp.float32, jnp.bfloat16
    place = lax.axis_index("exp")
    seq = lax.axis_index("seq")
    w_units = w_expert.shape[1]
    x, y = torus_place()
    loads = [
        pltpu.make_async_copy(source, target, local_sem.at[number])
        for number, (source, target) in enumerate(
            ((w_keyval_hbm, w_keyval), (w_query_hbm, w_query), (w_out_hbm, w_out))
        )
    ]
    for load in loads:
        load.start()
    weights[0, 0 : w_units] = w_expert[0]
    weights[0, w_units : 2 * w_units] = w_expert[1]
    weights[0, 2 * w_units :] = jnp.zeros_like(weights[0, 2 * w_units :])
    weights[0, 2 * w_units : 3 * w_units] = w_expert[2]
    greet(
        ring_partners()
        + [at_torus(x + dx, y + dy) for dx, dy in ((0, 1), (0, -1), (0, 2), (1, 0), (-1, 0))]
    )

    w_gather = TorusGather(lambda slot, quarter: weights.at[slot, :, pl.ds(quarter * 512, 512)], w_send, w_recv)

    w_gather.stage(0, range(4))
    row16 = lax.broadcasted_iota(jnp.int32, (16, 128), 0)
    tally = jnp.zeros((16, 128), f32)
    for device in range(16):
        tally = jnp.where(row16 == device, counts[device].astype(f32), tally)
    tallies[0] = tally

    def count_copy(shift):
        return remote(
            tallies.at[0], tallies.at[SIDE - shift], count_send.at[shift - 1], count_recv.at[shift - 1],
            at_torus(x, y + shift),
        )

    for shift in (1, 2, 3):
        count_copy(shift).start()
    acc[...] = jnp.zeros_like(acc)
    units_of[...] = jnp.zeros_like(units_of)

    mine = rows[pl.ds(place, 1), :]
    onehot = jnp.where(
        lax.broadcasted_iota(jnp.int32, (tokens.shape[0], SLOTS), 0) == mine, 1.0, 0.0
    ).T.astype(bf16)
    chosen = jnp.dot(onehot, tokens[...], preferred_element_type=f32)
    picked[...] = chosen.astype(bf16)
    gathered[place] = normalize(chosen, gains[0:1, :])
    ring_gather(gathered, g_send, g_recv, gs_send, gs_recv)
    for load in loads:
        load.wait()
    half_rows = SHARD // 2
    inputs = gathered[...].reshape(SHARD, WIDTH)
    keys = jnp.dot(inputs, w_keyval[0], preferred_element_type=f32).astype(bf16)
    values = jnp.dot(inputs, w_keyval[1], preferred_element_type=f32)
    values = (values * live_lanes(tally)).astype(bf16)
    kv[0, :, :, 0:HEAD_DIM] = keys.reshape(2, half_rows, HEAD_DIM)
    kv[0, :, :, HEAD_DIM:] = values.reshape(2, half_rows, HEAD_DIM)
    kv_gather = LineGather(1, lambda offset, half: kv.at[offset, half], kv_send, kv_recv)
    kv_gather.begin()
    queries = jnp.dot(inputs, w_query[...], preferred_element_type=f32).astype(bf16)
    query[0] = queries.reshape(2, half_rows, HEAD_DIM)
    q_gather = LineGather(0, lambda offset, half: query.at[offset, half], q_send, q_recv)
    q_gather.begin()

    c1 = HEAD_DIM ** (-0.5) / softcap_limit
    c2 = softcap_limit * math.log2(math.e)
    tile = 384

    def unit(dx, dy, diagonal=False):
        unit_keys = kv[dy, :, :, 0:HEAD_DIM].reshape(SHARD, HEAD_DIM)
        live = live_lanes(tallies[dy]).astype(bf16)
        unit_values = jnp.concatenate([kv[dy, :, :, HEAD_DIM:].reshape(SHARD, HEAD_DIM), live], axis=1)

        for half in range(2):

            @pl.loop(0, half_rows // tile)
            def _(number):
                first = pl.multiple_of(number * tile, tile)
                scores = lax.dot_general(
                    query[dx, half, pl.ds(first, tile), :], unit_keys, (((1,), (1,)), ((), ())),
                    preferred_element_type=f32,
                )
                weight = jnp.exp2(c2 * jnp.tanh(scores * c1))
                if diagonal:
                    row = lax.broadcasted_iota(jnp.int32, (tile, SHARD), 0) + first + half * half_rows
                    column = lax.broadcasted_iota(jnp.int32, (tile, SHARD), 1)
                    weight = jnp.where(column <= row, weight, 0.0)
                acc[dx, half, pl.ds(first, tile), :] += jnp.dot(
                    weight.astype(bf16), unit_values, preferred_element_type=f32
                )

    def earlier(dx, dy):
        @pl.when((wrap(x + dx, SIDE) > x) if dx else (wrap(y + dy, SIDE) < y))
        def _():
            unit(dx, dy)

    unit(0, 0, True)

    named_by = jnp.concatenate(
        [
            jnp.max(jnp.where(ids[...] == expert, 1.0, 0.0), axis=0, keepdims=True)
            for expert in range(16)
        ],
        axis=0,
    )
    named = jnp.max(jnp.where(ids[...] == place, 1.0, 0.0), axis=0, keepdims=True)
    before = jnp.where(
        lax.broadcasted_iota(jnp.int32, (SHARD, SHARD), 0) <= lax.broadcasted_iota(jnp.int32, (SHARD, SHARD), 1), 1.0, 0.0
    ).astype(bf16)
    named8 = jnp.broadcast_to(named, (16, SHARD))
    rank = jnp.dot(named8.astype(bf16), before, preferred_element_type=f32) * named8
    rank_column = rank.T[:, 0:1]
    capacity = routed.shape[0]
    select = jnp.where(
        lax.broadcasted_iota(jnp.int32, (capacity, SHARD), 0).astype(f32) + 1.0 == rank[0:1, :], 1.0, 0.0
    ).astype(bf16)
    spread = jnp.where(
        lax.broadcasted_iota(jnp.int32, (SHARD, capacity), 1).astype(f32) + 1.0 == rank_column, 1.0, 0.0
    ).astype(bf16)

    q_gather.forward()
    kv_gather.forward()
    earlier(1, 0)
    earlier(3, 0)
    for shift in (1, 2, 3):
        count_copy(shift).wait_recv()
    q_gather.last()
    earlier(2, 0)
    for dy in (1, 3):
        for dx in (2, 1, 3, 0):
            earlier(dx, dy)
    kv_gather.last()
    earlier(2, 2)

    def term_copies(direction, half, hop):
        number = (0 if direction > 0 else 3) + (hop if half == (0 if direction > 0 else 1) else 2)
        target = along(0, direction)
        return (
            remote(term_out.at[number], term_in.at[number], t_send.at[number], t_recv.at[number], target),
            remote(mass_out.at[number], mass_in.at[number], m_send.at[number], m_recv.at[number], target),
        ), number

    def send_terms(direction, half, hop, dx, received):
        copies, number = term_copies(direction, half, hop)
        value = acc[dx, half, :, 0:HEAD_DIM]
        mass = acc[dx, half, :, HEAD_DIM:].T[0:8, :]
        if received is not None:
            value = value + term_in[received].astype(f32)
            mass = mass + mass_in[received]
        term_out[number] = value.astype(bf16)
        mass_out[number] = mass
        for copy in copies:
            copy.start()

    def take_terms(direction, half, hop):
        copies, number = term_copies(direction, half, hop)
        for copy in copies:
            copy.wait_recv()
        return number

    send_terms(1, 0, 0, 2, None)
    send_terms(-1, 1, 0, 2, None)
    earlier(1, 2)
    earlier(3, 2)
    send_terms(1, 1, 0, 1, None)
    send_terms(-1, 0, 0, 3, None)
    send_terms(1, 0, 1, 1, take_terms(1, 0, 0))
    send_terms(-1, 1, 1, 3, take_terms(-1, 1, 0))
    w_gather.stage(1, range(4))
    earlier(0, 2)
    for half in range(2):
        value = acc[0, half, :, 0:HEAD_DIM]
        mass = acc[0, half, :, HEAD_DIM:]
        for direction in (-1, 1):
            number = take_terms(direction, half, 1 if half == (0 if direction > 0 else 1) else 0)
            value = value + term_in[number].astype(f32)
            mass = mass + jnp.broadcast_to(mass_in[number].T[:, 0:1], mass.shape)
        attended[half * half_rows : (half + 1) * half_rows, :] = (
            value / jnp.where(mass > 0, mass, 1.0)
        ).astype(bf16)

    @pl.loop(0, 4)
    def _(number):
        block = attended[pl.ds(pl.multiple_of(number * 4 * SLOTS, 4 * SLOTS), 4 * SLOTS), :]
        sums = jnp.dot(block, w_out[...], preferred_element_type=f32).astype(bf16)
        part[pl.ds(number * 4, 4)] = sums.reshape(4, SLOTS, WIDTH)

    def during_scatter(hop):
        pass

    def during_gather(hop):
        if hop == 1:
            w_gather.stage(2, (0,))
        if hop == 2:
            w_gather.stage(2, (2,))
        if hop == 3:
            w_gather.stage(2, (1,3))

    ring_scatter(part, sib, out_buf, in_buf, head, r_send, r_recv, rs_send, rs_recv, during_scatter)
    normed[place] = normalize(picked[...].astype(f32) + head[...], gains[1:2, :])
    ring_gather(normed, n_send, n_recv, ns_send, ns_recv, during_gather)

    everyone = normed[...].reshape(SHARD, WIDTH)
    routed[...] = jnp.dot(select, everyone, preferred_element_type=f32).astype(bf16)

    def experts(first, count):
        @pl.loop(0, count)
        def _(number):
            both = lax.dot_general(
                routed[...], weights[first + number, 0 : 2 * w_units], (((1,), (1,)), ((), ())),
                preferred_element_type=f32,
            )
            gated = both[:, 0:w_units]
            upward = both[:, w_units:]
            units_of[number, :, 0:w_units] = (gated / (1.0 + jnp.exp(-gated)) * upward).astype(bf16)

        down_rows = 3 * w_units + 8 - 2 * w_units

        @pl.loop(0, 4)
        def _(number):
            columns = pl.ds(pl.multiple_of(number * 512, 512), 512)
            blank = jnp.zeros((128 - down_rows, 512), bf16)
            left = jnp.concatenate([units_of[chunk] for chunk in range(count)], axis=1)
            right = jnp.concatenate(
                [
                    rows_of
                    for chunk in range(count)
                    for rows_of in (weights[first + chunk, 2 * w_units :, columns], blank)
                ],
                axis=0,
            )
            term = jnp.dot(left, right, preferred_element_type=f32)
            if first == 0:
                result[:, columns] = term
            else:
                result[:, columns] += term

    w_gather.arrive(4)
    experts(0, 5)
    w_gather.stage(3, range(4))
    w_gather.arrive(7, 10, 5)
    experts(5, 6)
    w_gather.arrive(13, 8, 11)
    experts(11, 4)
    scores = lax.dot_general(everyone, router[...], (((1,), (1,)), ((), ())), preferred_element_type=f32)
    scores = named_by.T / (1.0 + jnp.exp(-scores))
    own = jnp.where(lax.broadcasted_iota(jnp.int32, (SHARD, 16), 1) == place, scores, 0.0)
    share = jnp.sum(own, axis=1, keepdims=True) / jnp.sum(scores, axis=1, keepdims=True)
    w_gather.arrive(14)
    experts(15, 1)

    for column in range(4):
        columns = slice(column * 512, column * 512 + 512)
        term = jnp.dot(spread, result[:, columns].astype(bf16), preferred_element_type=f32) * share
        part[:, :, columns] = term.astype(bf16).reshape(16, SLOTS, 512)
    ring_scatter(part, sib2, out_buf2, in_buf2, total, b_send, b_recv, bs_send, bs_recv)
    live = lax.broadcasted_iota(jnp.int32, (SLOTS, 128), 0).astype(f32) < jnp.max(
        jnp.where(row16 == place, tally, 0.0), axis=0, keepdims=True
    )
    change = jnp.where(jnp.where(live, 1.0, 0.0)[:, 0:1] > 0, total[...] + head[...], 0.0)
    delta[...] = change
    logit = jnp.sum(picked[...].astype(f32) * depth_router[...].astype(f32), axis=1, keepdims=True)
    update = change / (1.0 + jnp.exp(-logit))
    high = update.astype(bf16)
    low = (update - high.astype(f32)).astype(bf16)
    back = jnp.where(lax.broadcasted_iota(jnp.int32, (tokens.shape[0], SLOTS), 0) == mine, 1.0, 0.0).astype(bf16)
    added = jnp.dot(back, high, preferred_element_type=f32) + jnp.dot(back, low, preferred_element_type=f32)
    mixed[...] = (tokens[...].astype(f32) + added).astype(bf16)

    for shift in (1, 2, 3):
        count_copy(shift).wait_send()
    for direction, half, hop in ((1, 0, 0), (1, 0, 1), (1, 1, 0), (-1, 1, 0), (-1, 1, 1), (-1, 0, 0)):
        for copy in term_copies(direction, half, hop)[0]:
            copy.wait_send()
    kv_gather.finish()
    q_gather.finish()
    w_gather.finish()


def dma(count):
    return pltpu.SemaphoreType.DMA((count,))


GATHER_SEMS = [dma(16), dma(16), dma(17), dma(17)]
SCATTER_BUFS = [
    pltpu.VMEM((RING, SLOTS, WIDTH), jnp.bfloat16),
    pltpu.VMEM((16, SLOTS, HALF), jnp.bfloat16),
    pltpu.VMEM((16, SLOTS, HALF), jnp.bfloat16),
]
SCATTER_SEMS = [dma(16), dma(16), dma(8), dma(8)]
SMEM = pl.BlockSpec(memory_space=pltpu.SMEM)
ANY = pl.BlockSpec(memory_space=pl.ANY)
CAPACITY = 416


def local(
    tokens, pick_rows, pick_counts, expert_ids, norm_gains, depth_router,
    w_query, w_keyval, w_out, expert_router, w_expert,
):
    f32, bf16 = jnp.float32, jnp.bfloat16
    units = w_expert.shape[3]
    return pl.pallas_call(
        block_kernel,
        out_shape=(
            jax.ShapeDtypeStruct(tokens.shape, bf16),
            jax.ShapeDtypeStruct((SLOTS, WIDTH), f32),
        ),
        in_specs=[VMEM, VMEM, SMEM] + [VMEM] * 3 + [ANY] * 3 + [VMEM] * 2,
        out_specs=(VMEM,) * 2,
        scratch_shapes=[
            pltpu.VMEM((WIDTH, HEAD_DIM), bf16),
            pltpu.VMEM((2, WIDTH, HEAD_DIM), bf16),
            pltpu.VMEM((HEAD_DIM, WIDTH), bf16),
            pltpu.VMEM((SLOTS, WIDTH), bf16),
            pltpu.VMEM((SLOTS, WIDTH), f32),
            pltpu.VMEM((16, SLOTS, WIDTH), bf16),
            pltpu.VMEM((SIDE, 2, SHARD // 2, 2 * HEAD_DIM), bf16),
            pltpu.VMEM((SIDE, 2, SHARD // 2, HEAD_DIM), bf16),
            pltpu.VMEM((SIDE, 16, 128), f32),
            pltpu.VMEM((SIDE, 2, SHARD // 2, 2 * HEAD_DIM), f32),
            pltpu.VMEM((6, SHARD // 2, HEAD_DIM), bf16),
            pltpu.VMEM((6, SHARD // 2, HEAD_DIM), bf16),
            pltpu.VMEM((6, 8, SHARD // 2), f32),
            pltpu.VMEM((6, 8, SHARD // 2), f32),
            pltpu.VMEM((SHARD, HEAD_DIM), bf16),
            pltpu.VMEM((16, 3 * units + 8, WIDTH), bf16),
            pltpu.VMEM((16, SLOTS, WIDTH), bf16),
        ]
        + SCATTER_BUFS
        + [
            pltpu.VMEM((SLOTS, WIDTH), f32),
            pltpu.VMEM((16, SLOTS, WIDTH), bf16),
            pltpu.VMEM((CAPACITY, WIDTH), bf16),
            pltpu.VMEM((6, CAPACITY, 128), bf16),
            pltpu.VMEM((CAPACITY, WIDTH), f32),
        ]
        + SCATTER_BUFS
        + [dma(3)]
        + GATHER_SEMS
        + [dma(6) for _ in range(8)]
        + [dma(3), dma(3), dma(60), dma(60)]
        + SCATTER_SEMS
        + GATHER_SEMS
        + SCATTER_SEMS,
        compiler_params=pltpu.CompilerParams(collective_id=0, has_side_effects=True, vmem_limit_bytes=60 << 20),
        name="block",
    )(
        tokens, pick_rows, pick_counts, expert_ids.T, norm_gains, depth_router[None, :], w_query, w_keyval, w_out,
        expert_router.T, jnp.transpose(w_expert[0], (0, 2, 1)),
    )


def solution(mesh):
    in_specs = (
        P(("seq", "exp"), None), P("seq", None), P("seq"), P("seq", None), P(), P(),
        P(None, "exp"), P(None, None, "exp"), P("exp", None), P(), P("exp", None, None, "seq"),
    )
    out_specs = (P(("seq", "exp"), None), P(("seq", "exp"), None))
    return jax.shard_map(local, mesh=mesh, in_specs=in_specs, out_specs=out_specs, check_vma=False)
```
